256 devices in a mesh: dom: 64 (over x, z, core), hid: 4 (over y).
Axes of the slice: x: 4, y: 4, z: 8, core: 2. Of those that a mesh axis runs over, the one named last changes fastest.
Arguments:
- features: bfloat16 [32768, 640], P('dom'), may hold values from -6 to 6
- self_weight: bfloat16 [640, 1024], P(None, 'hid'), may hold values from -0.25 to 0.25
- neigh_weight: bfloat16 [640, 1024], P(None, 'hid'), may hold values from -0.25 to 0.25
- cotangent: bfloat16 [32768, 1024], P('dom', 'hid'), may hold values from -6 to 6
- neighbor_blocks: int32 [64, 4, 8], P('dom'), may hold values from 0 to 3
- local_tiles: bfloat16 [64, 4, 8, 128, 128], P('dom'), may hold values from 0 to 1, as said below
- send_blocks: int32 [64, 4, 2], P('dom'), may hold values from 0 to 3
- recv_blocks: int32 [64, 4, 2], P('dom'), may hold values from 0 to 3
- live_slots: int32 [64, 4], P('dom'), may hold values from 1 to 2, as said below
- boundary_tiles: bfloat16 [64, 4, 2, 128, 128], P('dom'), may hold values from 0 to 1, as said below
Outputs:
- activated: bfloat16 [32768, 1024], P('dom', 'hid')
- grad_self: float32 [640, 1024], P(None, 'hid')
- grad_neigh: float32 [640, 1024], P(None, 'hid')
- grad_input: bfloat16 [32768, 640], P('dom', 'hid')
The draws below stay inside these ranges and needn't reach their ends.
Inputs may be any that keep to these rules, and one draw needn't show every extreme that they name: `local_tiles`: entries are 0 or 1; in the first of a block's 8 tiles every row holds a one. `boundary_tiles`: entries are 0 or 1. `live_slots`: slots at or beyond this count are padding; in every round some partition has 2 and some has 1.
All inputs are finite; a program needn't handle non-finite values.
Results may differ from the reference program's by a relative error of at most 0.006.
Values may be sent and summed in bfloat16 or wider, within the bound.
No kernel may reach another device: no remote copies, remote signals or barrier semaphores. Data moves between devices by JAX's collectives and lax.ppermute only.
A program may use at most 64 MiB of HBM per device.

```python
import math
import jax
import jax.numpy as jnp
from jax import lax

F = 640
H = 1024
BS = 128
BLK_DEV = 4
K_IN = 8
ROUNDS = 4
NB = 2
NODES = 32768
N_DOM = 64


def draw_local_tiles(key, part):
    key = jax.random.fold_in(key, 11)
    random_bits = jax.random.bernoulli(key, 0.125, (N_DOM, BLK_DEV, K_IN, BS, BS)).astype(jnp.float32)
    row_ids = jnp.arange(BS)[:, None]
    col_ids = jnp.arange(BS)[None, :]
    cycle = (col_ids == (row_ids + 1) % BS).astype(jnp.float32)
    leading = jnp.maximum(random_bits[:, :, :1], cycle)
    return jnp.concatenate([leading, random_bits[:, :, 1:]], axis=2).astype(jnp.bfloat16)


def draw_boundary_tiles(key, part):
    key = jax.random.fold_in(key, 12)
    random_bits = jax.random.bernoulli(key, 0.25, (N_DOM, ROUNDS, NB, BS, BS)).astype(jnp.float32)
    return random_bits.astype(jnp.bfloat16)


def draw_live_slots(key, part):
    key = jax.random.fold_in(key, 13)
    key_base, key_full, key_low = jax.random.split(key, 3)
    counts = jax.random.randint(key_base, (N_DOM, ROUNDS), 1, NB + 1)
    fullest = jax.random.randint(key_full, (ROUNDS,), 0, N_DOM)
    lowest = (fullest + 1 + jax.random.randint(key_low, (ROUNDS,), 0, N_DOM - 1)) % N_DOM
    domain_ids = jnp.arange(N_DOM)[:, None]
    counts = jnp.where(domain_ids == lowest[None, :], 1, counts)
    counts = jnp.where(domain_ids == fullest[None, :], NB, counts)
    return counts.astype(jnp.int32)


def plant(values, key, least, largest):
    index_at = [jax.random.randint(jax.random.fold_in(key, axis), (), 0, length) for axis, length in enumerate(values.shape)]
    main_axis = values.shape.index(max(values.shape))
    beside = index_at[:main_axis] + [(index_at[main_axis] + 1) % values.shape[main_axis]] + index_at[main_axis + 1:]
    return values.at[tuple(index_at)].set(least).at[tuple(beside)].set(largest)


def steps_of(stream_key, dims, shards, smallest, high):
    def one(axis_at, parts):
        draws = jax.random.uniform(jax.random.fold_in(jax.random.fold_in(stream_key, 6), axis_at), (parts,), jnp.float32, smallest / len(shards), high / len(shards))
        return jnp.repeat(jnp.exp(draws), dims[axis_at] // parts).reshape((-1,) + (1,) * (len(dims) - axis_at - 1))

    loudness = one(*shards[0])
    for cut in shards[1:]:
        loudness = loudness * one(*cut)
    return loudness


def scatter_about(key, dims, width, bound, cuts=(), dtype=jnp.bfloat16):
    entries = width * jax.random.normal(key, dims, jnp.float32)
    if cuts:
        entries = entries * steps_of(key, dims, cuts, -0.22, 0.18)
    return jnp.clip(entries, -bound, bound).astype(dtype)


def setup_inputs(seed: int = 0) -> dict:
    keys = jax.random.split(jax.random.key(seed), 11)
    return {
        "features": scatter_about(keys[0], (NODES, F), 1.0, 6.0, ((0, 64),)),
        "self_weight": scatter_about(keys[1], (F, H), F ** -0.5, 0.25, ((1, 4),)),
        "neigh_weight": scatter_about(keys[2], (F, H), F ** -0.5, 0.25, ((1, 4),)),
        "cotangent": scatter_about(keys[3], (NODES, H), 1.0, 6.0, ((0, 64), (1, 4))),
        "neighbor_blocks": plant(jax.random.randint(keys[4], (N_DOM, BLK_DEV, K_IN), 0, BLK_DEV), jax.random.fold_in(keys[4], 1), 0, BLK_DEV - 1).astype(jnp.int32),
        "local_tiles": draw_local_tiles(jax.random.fold_in(keys[10], 71), 0),
        "send_blocks": plant(jax.random.randint(keys[6], (N_DOM, ROUNDS, NB), 0, BLK_DEV), jax.random.fold_in(keys[6], 1), 0, BLK_DEV - 1).astype(jnp.int32),
        "recv_blocks": plant(jax.random.randint(keys[7], (N_DOM, ROUNDS, NB), 0, BLK_DEV), jax.random.fold_in(keys[7], 1), 0, BLK_DEV - 1).astype(jnp.int32),
        "live_slots": draw_live_slots(jax.random.fold_in(keys[10], 71), 0),
        "boundary_tiles": draw_boundary_tiles(jax.random.fold_in(keys[10], 71), 0),
    }


def round_offsets():
    return [(round_index // 2 + 1) * (1 - 2 * (round_index % 2)) for round_index in range(ROUNDS)]

def reference(features, self_weight, neigh_weight, cotangent, neighbor_blocks, local_tiles, send_blocks, recv_blocks, live_slots, boundary_tiles):
    grouped = features.reshape(N_DOM, BLK_DEV, BS, F)
    domain_index = jnp.arange(N_DOM)[:, None]
    slot_range = jnp.arange(NB)[None, :]
    offsets = round_offsets()
    degree = lax.optimization_barrier(jnp.sum(local_tiles.astype(jnp.float32), axis=(2, 4)))
    summed = jnp.zeros((N_DOM, BLK_DEV, BS, F), jnp.float32)
    for neighbor_slot in range(K_IN):
        picked = jnp.take_along_axis(grouped, neighbor_blocks[:, :, neighbor_slot][:, :, None, None], axis=1)
        summed = summed + jnp.einsum('dbij,dbjf->dbif', local_tiles[:, :, neighbor_slot].astype(jnp.float32), picked.astype(jnp.float32))
    masked_all = []
    for round_index in range(ROUNDS):
        live_mask = (slot_range < live_slots[:, round_index][:, None]).astype(jnp.float32)
        live_tiles = boundary_tiles[:, round_index].astype(jnp.float32) * live_mask[:, :, None, None]
        masked_all.append(live_tiles)
        outgoing = jnp.take_along_axis(grouped, send_blocks[:, round_index][:, :, None, None], axis=1)
        received = jnp.roll(outgoing, offsets[round_index], axis=0)
        contribution = jnp.einsum('dsij,dsjf->dsif', live_tiles, received.astype(jnp.float32))
        summed = summed.at[domain_index, recv_blocks[:, round_index]].add(contribution)
        degree = degree.at[domain_index, recv_blocks[:, round_index]].add(lax.optimization_barrier(jnp.sum(live_tiles, axis=3)))
    mean_rows = (summed / degree[..., None]).reshape(NODES, F)
    preact = jnp.dot(features, self_weight, preferred_element_type=jnp.float32) + jnp.dot(mean_rows, neigh_weight.astype(jnp.float32), precision=lax.Precision.HIGHEST)
    activated = jax.nn.silu(preact).astype(jnp.bfloat16)
    sigmoid_z = jax.nn.sigmoid(preact)
    grad_pre = cotangent.astype(jnp.float32) * sigmoid_z * (1.0 + preact * (1.0 - sigmoid_z))
    grad_low = grad_pre.astype(jnp.bfloat16)
    spread = (grad_pre / degree.reshape(NODES)[:, None]).astype(jnp.bfloat16).reshape(N_DOM, BLK_DEV, BS, H)
    back_sum = jnp.zeros((N_DOM, BLK_DEV, BS, H), jnp.float32)
    for neighbor_slot in range(K_IN):
        term = jnp.einsum('dbij,dbih->dbjh', local_tiles[:, :, neighbor_slot].astype(jnp.float32), spread.astype(jnp.float32))
        back_sum = back_sum.at[domain_index, neighbor_blocks[:, :, neighbor_slot]].add(term)
    for round_index in range(ROUNDS):
        picked = jnp.take_along_axis(spread, recv_blocks[:, round_index][:, :, None, None], axis=1)
        term = jnp.einsum('dsij,dsih->dsjh', masked_all[round_index], picked.astype(jnp.float32))
        returned = jnp.roll(term, -offsets[round_index], axis=0)
        back_sum = back_sum.at[domain_index, send_blocks[:, round_index]].add(returned)
    back_rows = back_sum.astype(jnp.bfloat16).reshape(NODES, H)
    grad_scale = 1.0 / math.sqrt(NODES)
    grad_self = jnp.dot(features.T, grad_low, preferred_element_type=jnp.float32) * grad_scale
    grad_neigh = jnp.dot(features.T, back_rows, preferred_element_type=jnp.float32) * grad_scale
    grad_input = (jnp.dot(grad_low, self_weight.T, preferred_element_type=jnp.float32) + jnp.dot(back_rows, neigh_weight.T, preferred_element_type=jnp.float32)).astype(jnp.bfloat16)
    return (activated, grad_self, grad_neigh, grad_input)
```

```python
import functools
import math

import jax
import jax.numpy as jnp
from jax import lax
from jax.experimental import pallas as pl
from jax.experimental.pallas import tpu as pltpu
from jax.sharding import PartitionSpec as P

BS = 128
BLK = 4
K_IN = 8
ROUNDS = 4
NB = 2
CORES = 2
Z = 8
X = 4
HID = 4
OFFSETS = (1, -1, 2, -2)
BF16 = jnp.bfloat16
F32 = jnp.float32

VMEM = pl.BlockSpec(memory_space=pltpu.VMEM)
SMEM = pl.BlockSpec(memory_space=pltpu.SMEM)


def dot(a, b, dims=((1,), (0,))):
    return lax.dot_general(a, b, (dims, ((), ())), preferred_element_type=F32)


def call(kernel, outs, specs, flops=0, nbytes=0, limit=24, scratch=()):
    return pl.pallas_call(
        kernel,
        out_shape=[jax.ShapeDtypeStruct(shape, dtype) for shape, dtype in outs],
        in_specs=specs,
        out_specs=[VMEM] * len(outs),
        scratch_shapes=list(scratch),
        compiler_params=pltpu.CompilerParams(vmem_limit_bytes=limit * 1024 * 1024),
        cost_estimate=pl.CostEstimate(flops=flops, bytes_accessed=nbytes, transcendentals=0),
    )


def dom_shift(array, by):
    count = lax.axis_size("dom")
    return lax.ppermute(array, "dom", [(i, (i + by) % count) for i in range(count)])


def dom_swap(array, mask):
    count = lax.axis_size("dom")
    return lax.ppermute(array, "dom", [(i, i ^ mask) for i in range(count)])


def hid_swap(array, mask):
    return lax.ppermute(array, "hid", [(i, i ^ mask) for i in range(HID)])


def rows(block, size=BS):
    return pl.ds(pl.multiple_of(block * size, size), size)


def pack_kernel(send, feats, *outs):
    for r in range(ROUNDS):
        for s in range(NB):
            outs[r][s * BS : (s + 1) * BS, :] = feats[rows(send[0, r, s]), :]


def before_kernel(
    neighbors, recv, live, feats, self_w, tiles, edge_tiles, local, edge, local_sum, degree, own_pre
):
    local[...] = jnp.zeros_like(local)
    edge[...] = jnp.zeros_like(edge)
    for b in range(BLK):
        for k in range(K_IN):
            cols = rows(neighbors[0, b, k])
            here = slice(b * BS, (b + 1) * BS)
            local[here, cols] = local[here, cols] + tiles[0, b, k]
    for r in range(ROUNDS):
        for s in range(NB):
            slot = r * NB + s

            @pl.when(s < live[0, r])
            def _():
                edge[rows(recv[0, r, s]), slot * BS : (slot + 1) * BS] = edge_tiles[0, r, s]

    feats_now = feats[...]
    own_pre[...] = dot(feats_now, self_w[...])
    local_now = local[...]
    local_sum[...] = dot(local_now, feats_now)
    ones = jnp.ones((BS * BLK, BS), BF16)
    edge_ones = jnp.ones((BS * NB * ROUNDS, BS), BF16)
    degree[...] = dot(local_now, ones) + dot(edge[...], edge_ones)


def middle_kernel(
    edge,
    got0,
    got1,
    got2,
    got3,
    local_sum,
    degree,
    own_pre,
    neigh_w,
    cot,
    feats,
    activated,
    low_out,
    spread_out,
    keep,
    give,
    term0,
    term1,
    term2,
    term3,
):
    core = lax.rem(lax.axis_index("dom"), CORES)
    width = NB * BS
    total = local_sum[...]
    for r, got in enumerate((got0, got1, got2, got3)):
        total = total + dot(edge[:, r * width : (r + 1) * width], got[...])
    inverse = 1.0 / degree[...]
    mean = total * jnp.concatenate([inverse] * (total.shape[1] // BS), axis=1)
    mean_high = mean.astype(BF16)
    mean_rest = (mean - mean_high.astype(F32)).astype(BF16)
    weights = neigh_w[...]
    pre = own_pre[...] + dot(mean_high, weights) + dot(mean_rest, weights)
    sig = jax.nn.sigmoid(pre)
    activated[...] = (pre * sig).astype(BF16)
    grad = cot[...].astype(F32) * sig * (1.0 + pre * (1.0 - sig))
    low = grad.astype(BF16)
    low_out[...] = low
    spread = (grad * jnp.concatenate([inverse] * (grad.shape[1] // BS), axis=1)).astype(BF16)
    spread_out[...] = spread
    over_rows = ((0,), (0,))
    of_self = dot(feats[...], low, over_rows)
    of_neigh = dot(mean_high, low, over_rows)

    @pl.when(core == 0)
    def _():
        keep[...] = of_self
        give[...] = of_neigh.astype(BF16)

    @pl.when(core == 1)
    def _():
        keep[...] = of_neigh
        give[...] = of_self.astype(BF16)

    for r, term in enumerate((term0, term1, term2, term3)):
        term[...] = dot(edge[:, r * width : (r + 1) * width], spread, over_rows).astype(BF16)


def z_index():
    return lax.rem(lax.axis_index("dom") // CORES, Z)


def cut_kernel(keep, got, own, *gives):
    z = z_index()
    size = own.shape[0]
    own[...] = keep[rows(z, size), :] + got[rows(z, size), :].astype(F32)
    for k in range(1, Z):
        at = rows(jnp.bitwise_xor(z, k), size)
        gives[k - 1][...] = (keep[at, :] + got[at, :].astype(F32)).astype(BF16)


def add_kernel(own, *refs):
    total = own[...]
    for got in refs[:-1]:
        total = total + got[...].astype(F32)
    refs[-1][...] = total.astype(BF16)


def pair_kernel(a, b, c, d, out):
    out[...] = (
        (a[...].astype(F32) + b[...].astype(F32)) + (c[...].astype(F32) + d[...].astype(F32))
    ).astype(BF16)


def join_kernel(own, *refs):
    z = z_index()
    size = own.shape[0]
    out = refs[-1]
    out[rows(z, size), :] = own[...]
    for k in range(1, Z):
        out[rows(jnp.bitwise_xor(z, k), size), :] = refs[k - 1][...]


def last_kernel(scale, mine, other, of_self, of_neigh):
    core = lax.rem(lax.axis_index("dom"), CORES)

    @pl.when(core == 0)
    def _():
        of_self[...] = mine[...].astype(F32) * scale
        of_neigh[...] = other[...].astype(F32) * scale

    @pl.when(core == 1)
    def _():
        of_self[...] = other[...].astype(F32) * scale
        of_neigh[...] = mine[...].astype(F32) * scale


def back_kernel(
    send, local, spread, got0, got1, got2, got3, low, self_w, neigh_w, own, give1, give2, give3, back
):
    back[...] = dot(local[...], spread[...], ((0,), (0,)))
    for r, got in enumerate((got0, got1, got2, got3)):
        for s in range(NB):
            at = rows(send[0, r, s])
            back[at, :] = back[at, :] + got[s * BS : (s + 1) * BS, :].astype(F32)
    back_low = back[...].astype(BF16)
    low_now = low[...]
    y = lax.axis_index("hid")
    size = own.shape[0]
    over_hidden = ((1,), (1,))
    for k in range(HID):
        at = rows(jnp.bitwise_xor(y, k), size)
        part = dot(self_w[at, :], low_now, over_hidden) + dot(neigh_w[at, :], back_low, over_hidden)
        if k == 0:
            own[...] = part
        else:
            (give1, give2, give3)[k - 1][...] = part.astype(BF16)


def on_device(
    features,
    self_weight,
    neigh_weight,
    cotangent,
    neighbor_blocks,
    local_tiles,
    send_blocks,
    recv_blocks,
    live_slots,
    boundary_tiles,
):
    n, width = features.shape
    hidden = self_weight.shape[1]
    slots = ROUNDS * NB * BS
    packed = call(pack_kernel, [((NB * BS, width), BF16)] * ROUNDS, [SMEM, VMEM], nbytes=2_000_000)(
        send_blocks, features
    )
    received = [dom_shift(packed[r], OFFSETS[r]) for r in range(ROUNDS)]
    local, edge, local_sum, degree, own_pre = call(
        before_kernel,
        [((n, n), BF16), ((n, slots), BF16), ((n, width), F32), ((n, BS), F32), ((n, hidden), F32)],
        [SMEM] * 3 + [VMEM] * 4,
        flops=1_000_000_000,
        nbytes=6_000_000,
    )(
        neighbor_blocks,
        recv_blocks,
        live_slots,
        features,
        self_weight,
        local_tiles,
        boundary_tiles,
    )
    activated, low, spread, keep, give, *terms = call(
        middle_kernel,
        [((n, hidden), BF16)] * 3
        + [((width, hidden), F32), ((width, hidden), BF16)]
        + [((NB * BS, hidden), BF16)] * ROUNDS,
        [VMEM] * 11,
        flops=1_600_000_000,
        nbytes=8_000_000,
        limit=32,
    )(edge, *received, local_sum, degree, own_pre, neigh_weight, cotangent, features)

    got = dom_swap(give, 1)
    piece = (width // Z, hidden)
    own, *gives = call(
        cut_kernel, [(piece, F32)] + [(piece, BF16)] * (Z - 1), [VMEM] * 2, nbytes=1_500_000
    )(keep, got)
    pieces = [dom_swap(gives[k - 1], CORES * k) for k in range(1, Z)]
    returned = [dom_shift(terms[r], -OFFSETS[r]) for r in range(ROUNDS)]
    (part,) = call(add_kernel, [(piece, BF16)], [VMEM] * Z, nbytes=400_000)(own, *pieces)
    across = [dom_swap(part, CORES * Z * k) for k in range(1, X)]
    (done,) = call(pair_kernel, [(piece, BF16)], [VMEM] * X, nbytes=200_000)(part, *across)
    gathered = [dom_swap(done, CORES * k) for k in range(1, Z)]
    shape = (width // HID, n)
    in_own, *in_gives = call(
        back_kernel,
        [(shape, F32)] + [(shape, BF16)] * (HID - 1),
        [SMEM] + [VMEM] * 9,
        flops=600_000_000,
        nbytes=3_000_000,
        scratch=[pltpu.VMEM((n, hidden), F32)],
    )(send_blocks, local, spread, *returned, low, self_weight, neigh_weight)
    in_parts = [hid_swap(in_gives[k - 1], k) for k in range(1, HID)]
    (mine,) = call(join_kernel, [((width, hidden), BF16)], [VMEM] * Z, nbytes=700_000)(
        done, *gathered
    )
    other = dom_swap(mine, 1)
    scale = 1.0 / math.sqrt(n * lax.axis_size("dom"))
    grad_self, grad_neigh = call(
        functools.partial(last_kernel, scale),
        [((width, hidden), F32)] * 2,
        [VMEM] * 2,
        nbytes=2_000_000,
    )(mine, other)
    grad_input = in_own
    for part in in_parts:
        grad_input = grad_input + part.astype(F32)
    return activated, grad_self, grad_neigh, grad_input.astype(BF16).T


def solution(mesh):
    return jax.shard_map(
        on_device,
        mesh=mesh,
        in_specs=(
            P("dom", None),
            P(None, "hid"),
            P(None, "hid"),
            P("dom", "hid"),
            P("dom", None, None),
            P("dom", None, None, None, None),
            P("dom", None, None),
            P("dom", None, None),
            P("dom", None),
            P("dom", None, None, None, None),
        ),
        out_specs=(P("dom", "hid"), P(None, "hid"), P(None, "hid"), P("dom", "hid")),
        check_vma=False,
    )
```

```python
import functools
import math

import jax
import jax.numpy as jnp
from jax import lax
from jax.experimental import pallas as pl
from jax.experimental.pallas import tpu as pltpu
from jax.sharding import PartitionSpec as P

BS = 128
BLK = 4
K_IN = 8
ROUNDS = 4
NB = 2
CORES = 2
Z = 8
X = 4
HID = 4
CHIPS = X * Z
PIECE = (40, 128)
BF16 = jnp.bfloat16
F32 = jnp.float32

VMEM = pl.BlockSpec(memory_space=pltpu.VMEM)
HBM = pl.BlockSpec(memory_space=pltpu.MemorySpace.HBM)
DMA = pltpu.SemaphoreType.DMA


def dot(a, b, dims=((1,), (0,))):
    return lax.dot_general(a, b, (dims, ((), ())), preferred_element_type=F32)


def call(kernel, outs, specs, flops=0, nbytes=0, limit=24, scratch=()):
    return pl.pallas_call(
        kernel,
        out_shape=[jax.ShapeDtypeStruct(shape, dtype) for shape, dtype in outs],
        in_specs=specs,
        out_specs=[VMEM] * len(outs),
        scratch_shapes=list(scratch),
        compiler_params=pltpu.CompilerParams(vmem_limit_bytes=limit * 1024 * 1024),
        cost_estimate=pl.CostEstimate(flops=flops, bytes_accessed=nbytes, transcendentals=0),
    )


def dom_swap(array, mask):
    count = lax.axis_size("dom")
    return lax.ppermute(array, "dom", [(i, i ^ mask) for i in range(count)])


def dom_pairs(array, step):
    count = lax.axis_size("dom")
    odd = [i for i in range(count) if (i // step) % 2]
    pairs = [(i, (i + step) % count) for i in odd]
    return lax.ppermute(array, "dom", pairs + [(j, i) for i, j in pairs])


def hid_swap(array, mask):
    return lax.ppermute(array, "hid", [(i, i ^ mask) for i in range(HID)])


def exchange(array):
    groups = [[CORES * chip + core for chip in range(CHIPS)] for core in range(CORES)]
    return lax.all_to_all(array, "dom", 0, 0, axis_index_groups=groups)


def rows(block, size=BS):
    return pl.ds(pl.multiple_of(block * size, size), size)


def swaps(arrays):
    a, b, c, d = arrays
    return [dom_swap(a, 1), dom_swap(b, 2), dom_pairs(c, 2), dom_pairs(d, 1)]


def sent_rounds():
    me = lax.axis_index("dom")
    core, chip = lax.rem(me, CORES), lax.rem(me // CORES, 2)
    return (core, 2 + chip, 3 - chip, 1 - core)


def received_rounds():
    first, second, third, fourth = sent_rounds()
    return (1 - first, 5 - second, 5 - third, 1 - fourth)


def pack_kernel(send, feats, out0, out1, out2, out3, send_now, sems):
    copy = pltpu.make_async_copy(send, send_now, sems.at[ROUNDS * NB])
    copy.start()
    copy.wait()
    copies = []
    for i, (r, out) in enumerate(zip(sent_rounds(), (out0, out1, out2, out3))):
        for s in range(NB):
            copies.append(
                pltpu.make_async_copy(
                    feats.at[rows(send_now[0, s, r]), :],
                    out.at[pl.ds(s * BS, BS), :],
                    sems.at[i * NB + s],
                )
            )
            copies[-1].start()
    for copy in copies:
        copy.wait()


def before_kernel(
    neighbors,
    recv,
    live,
    feats,
    self_w,
    tiles,
    edge_tiles,
    local,
    edge,
    local_sum,
    degree,
    own_pre,
    neighbors_now,
    recv_now,
    live_now,
    feats_now,
    self_w_now,
    tiles_now,
    edge_tiles_now,
    sems,
):
    pairs = (
        (neighbors, neighbors_now),
        (recv, recv_now),
        (live, live_now),
        (tiles, tiles_now),
        (edge_tiles, edge_tiles_now),
        (feats, feats_now),
        (self_w, self_w_now),
    )
    copies = [pltpu.make_async_copy(a, b, sems.at[i]) for i, (a, b) in enumerate(pairs)]
    for copy in copies:
        copy.start()
    local[...] = jnp.zeros_like(local)
    edge[...] = jnp.zeros_like(edge)
    for copy in copies:
        copy.wait()
    for b in range(BLK):
        for k in range(K_IN):
            cols = rows(neighbors_now[0, b, k])
            here = slice(b * BS, (b + 1) * BS)
            local[here, cols] = local[here, cols] + tiles_now[0, b, k]
    for i, r in enumerate(received_rounds()):
        for s in range(NB):
            slot = i * NB + s

            @pl.when(s < live_now[0, r])
            def _():
                edge[rows(recv_now[0, s, r]), slot * BS : (slot + 1) * BS] = edge_tiles_now[0, r, s]

    mine = feats_now[...]
    own_pre[...] = dot(mine, self_w_now[...])
    whole = local[...]
    local_sum[...] = dot(whole, mine)
    ones = jnp.ones((BS * BLK, BS), BF16)
    edge_ones = jnp.ones((BS * NB * ROUNDS, BS), BF16)
    degree[...] = dot(whole, ones) + dot(edge[...], edge_ones)


def middle_kernel(
    edge,
    got0,
    got1,
    got2,
    got3,
    local_sum,
    degree,
    own_pre,
    neigh_w,
    cot,
    feats,
    activated,
    low_out,
    spread_out,
    keep,
    give,
    term0,
    term1,
    term2,
    term3,
):
    core = lax.rem(lax.axis_index("dom"), CORES)
    width = NB * BS
    total = local_sum[...]
    for r, got in enumerate((got0, got1, got2, got3)):
        total = total + dot(edge[:, r * width : (r + 1) * width], got[...])
    inverse = 1.0 / degree[...]
    mean = total * jnp.concatenate([inverse] * (total.shape[1] // BS), axis=1)
    mean_high = mean.astype(BF16)
    mean_rest = (mean - mean_high.astype(F32)).astype(BF16)
    weights = neigh_w[...]
    pre = own_pre[...] + dot(mean_high, weights) + dot(mean_rest, weights)
    sig = jax.nn.sigmoid(pre)
    activated[...] = (pre * sig).astype(BF16)
    grad = cot[...].astype(F32) * sig * (1.0 + pre * (1.0 - sig))
    low = grad.astype(BF16)
    low_out[...] = low
    spread = (grad * jnp.concatenate([inverse] * (grad.shape[1] // BS), axis=1)).astype(BF16)
    spread_out[...] = spread
    over_rows = ((0,), (0,))
    of_self = dot(feats[...], low, over_rows)
    of_neigh = dot(mean_high, low, over_rows)

    @pl.when(core == 0)
    def _():
        keep[...] = of_self
        give[...] = of_neigh.astype(BF16)

    @pl.when(core == 1)
    def _():
        keep[...] = of_neigh
        give[...] = of_self.astype(BF16)

    for r, term in enumerate((term0, term1, term2, term3)):
        term[...] = dot(edge[:, r * width : (r + 1) * width], spread, over_rows).astype(BF16)


def piece_at(i):
    return (i % 16) * PIECE[0], (i // 16) * PIECE[1]


def cut_kernel(keep, got, out):
    total = keep[...] + got[...].astype(F32)
    for i in range(CHIPS):
        at, lane = piece_at(i)
        out[i] = total[at : at + PIECE[0], lane : lane + PIECE[1]].astype(BF16)


def sum_kernel(got, out):
    done = jnp.sum(got[...].astype(F32), axis=0).astype(BF16)
    for i in range(CHIPS):
        out[i] = done


def last_kernel(scale, mine, other, of_self, of_neigh):
    core = lax.rem(lax.axis_index("dom"), CORES)

    def put(a, out):
        for i in range(CHIPS):
            at, lane = piece_at(i)
            out[at : at + PIECE[0], lane : lane + PIECE[1]] = a[i].astype(F32) * scale

    @pl.when(core == 0)
    def _():
        put(mine, of_self)
        put(other, of_neigh)

    @pl.when(core == 1)
    def _():
        put(other, of_self)
        put(mine, of_neigh)


def back_own_kernel(local, spread, low, self_w, back, part):
    back[...] = dot(local[...], spread[...], ((0,), (0,)))
    part[...] = dot(self_w[...], low[...], ((1,), (1,)))


def back_kernel(send, start, part, got0, got1, got2, got3, neigh_w, own, give1, give2, give3, back):
    back[...] = start[...]
    for r, got in zip(sent_rounds(), (got0, got1, got2, got3)):
        for s in range(NB):
            at = rows(send[0, s, r])
            back[at, :] = back[at, :] + got[s * BS : (s + 1) * BS, :].astype(F32)
    back_low = back[...].astype(BF16)
    y = lax.axis_index("hid")
    size = own.shape[0]
    for k in range(HID):
        at = rows(jnp.bitwise_xor(y, k), size)
        total = part[at, :] + dot(neigh_w[at, :], back_low, ((1,), (1,)))
        if k == 0:
            own[...] = total
        else:
            (give1, give2, give3)[k - 1][...] = total.astype(BF16)


def on_device(
    features,
    self_weight,
    neigh_weight,
    cotangent,
    neighbor_blocks,
    local_tiles,
    send_blocks,
    recv_blocks,
    live_slots,
    boundary_tiles,
):
    n, width = features.shape
    hidden = self_weight.shape[1]
    slots = ROUNDS * NB * BS
    send_blocks = jnp.swapaxes(send_blocks, 1, 2)
    recv_blocks = jnp.swapaxes(recv_blocks, 1, 2)
    packed = call(
        pack_kernel,
        [((NB * BS, width), BF16)] * ROUNDS,
        [HBM] * 2,
        nbytes=2_000_000,
        scratch=[pltpu.SMEM((1, NB, ROUNDS), jnp.int32), DMA((ROUNDS * NB + 1,))],
    )(send_blocks, features)
    received = swaps(packed)
    local, edge, local_sum, degree, own_pre = call(
        before_kernel,
        [((n, n), BF16), ((n, slots), BF16), ((n, width), F32), ((n, BS), F32), ((n, hidden), F32)],
        [HBM] * 7,
        flops=1_000_000_000,
        nbytes=6_000_000,
        scratch=[
            pltpu.SMEM((1, BLK, K_IN), jnp.int32),
            pltpu.SMEM((1, NB, ROUNDS), jnp.int32),
            pltpu.SMEM((1, ROUNDS), jnp.int32),
            pltpu.VMEM((n, width), BF16),
            pltpu.VMEM((width, hidden), BF16),
            pltpu.VMEM((1, BLK, K_IN, BS, BS), BF16),
            pltpu.VMEM((1, ROUNDS, NB, BS, BS), BF16),
            DMA((7,)),
        ],
    )(
        neighbor_blocks,
        recv_blocks,
        live_slots,
        features,
        self_weight,
        local_tiles,
        boundary_tiles,
    )
    activated, low, spread, keep, give, *terms = call(
        middle_kernel,
        [((n, hidden), BF16)] * 3
        + [((width, hidden), F32), ((width, hidden), BF16)]
        + [((NB * BS, hidden), BF16)] * ROUNDS,
        [VMEM] * 11,
        flops=1_600_000_000,
        nbytes=8_000_000,
        limit=32,
    )(edge, *received, local_sum, degree, own_pre, neigh_weight, cotangent, features)

    got = dom_swap(give, 1)
    returned = swaps(terms)
    back, in_part = call(
        back_own_kernel,
        [((n, hidden), F32), ((width, n), F32)],
        [VMEM] * 4,
        flops=300_000_000,
        nbytes=3_000_000,
    )(local, spread, low, self_weight)
    got, back, in_part = lax.optimization_barrier((got, back, in_part))
    pieces = (CHIPS,) + PIECE
    (cut,) = call(cut_kernel, [(pieces, BF16)], [VMEM] * 2, nbytes=1_500_000)(keep, got)
    (summed,) = call(sum_kernel, [(pieces, BF16)], [VMEM], nbytes=700_000)(exchange(cut))
    shape = (width // HID, n)
    in_own, *in_gives = call(
        back_kernel,
        [(shape, F32)] + [(shape, BF16)] * (HID - 1),
        [pl.BlockSpec(memory_space=pltpu.SMEM)] + [VMEM] * 7,
        flops=300_000_000,
        nbytes=3_000_000,
        scratch=[pltpu.VMEM((n, hidden), F32)],
    )(send_blocks, back, in_part, *returned, neigh_weight)
    summed, *in_gives = lax.optimization_barrier((summed, *in_gives))
    in_parts = [hid_swap(in_gives[k - 1], k) for k in range(1, HID)]
    mine = exchange(summed)
    other = dom_swap(mine, 1)
    scale = 1.0 / math.sqrt(n * lax.axis_size("dom"))
    grad_self, grad_neigh = call(
        functools.partial(last_kernel, scale),
        [((width, hidden), F32)] * 2,
        [VMEM] * 2,
        nbytes=2_000_000,
    )(mine, other)
    grad_input = in_own
    for part in in_parts:
        grad_input = grad_input + part.astype(F32)
    return activated, grad_self, grad_neigh, grad_input.astype(BF16).T


def solution(mesh):
    return jax.shard_map(
        on_device,
        mesh=mesh,
        in_specs=(
            P("dom", None),
            P(None, "hid"),
            P(None, "hid"),
            P("dom", "hid"),
            P("dom", None, None),
            P("dom", None, None, None, None),
            P("dom", None, None),
            P("dom", None, None),
            P("dom", None),
            P("dom", None, None, None, None),
        ),
        out_specs=(P("dom", "hid"), P(None, "hid"), P(None, "hid"), P("dom", "hid")),
        check_vma=False,
    )
```

```python
import functools
import math

import jax
import jax.numpy as jnp
from jax import lax
from jax.experimental import pallas as pl
from jax.experimental.pallas import tpu as pltpu
from jax.sharding import PartitionSpec as P

BS = 128
BLK = 4
K_IN = 8
ROUNDS = 4
NB = 2
CORES = 2
Z = 8
X = 4
HID = 4
CHIPS = X * Z
PIECE = (40, 128)
BF16 = jnp.bfloat16
F32 = jnp.float32

VMEM = pl.BlockSpec(memory_space=pltpu.VMEM)
HBM = pl.BlockSpec(memory_space=pltpu.MemorySpace.HBM)
DMA = pltpu.SemaphoreType.DMA


def dot(a, b, dims=((1,), (0,))):
    return lax.dot_general(a, b, (dims, ((), ())), preferred_element_type=F32)


def call(kernel, outs, specs, flops=0, nbytes=0, limit=24, scratch=()):
    return pl.pallas_call(
        kernel,
        out_shape=[jax.ShapeDtypeStruct(shape, dtype) for shape, dtype in outs],
        in_specs=specs,
        out_specs=[VMEM] * len(outs),
        scratch_shapes=list(scratch),
        compiler_params=pltpu.CompilerParams(vmem_limit_bytes=limit * 1024 * 1024),
        cost_estimate=pl.CostEstimate(flops=flops, bytes_accessed=nbytes, transcendentals=0),
    )


def dom_swap(array, mask):
    count = lax.axis_size("dom")
    return lax.ppermute(array, "dom", [(i, i ^ mask) for i in range(count)])


def dom_pairs(array, step):
    count = lax.axis_size("dom")
    odd = [i for i in range(count) if (i // step) % 2]
    pairs = [(i, (i + step) % count) for i in odd]
    return lax.ppermute(array, "dom", pairs + [(j, i) for i, j in pairs])


def hid_swap(array, mask):
    return lax.ppermute(array, "hid", [(i, i ^ mask) for i in range(HID)])


def exchange(array):
    groups = [[CORES * chip + core for chip in range(CHIPS)] for core in range(CORES)]
    return lax.all_to_all(array, "dom", 0, 0, axis_index_groups=groups)


def in_hbm(array):
    return pltpu.with_memory_space_constraint(array, pltpu.MemorySpace.HBM)


def rows(block, size=BS):
    return pl.ds(pl.multiple_of(block * size, size), size)


def swaps(arrays):
    a, b, c, d = arrays
    return [dom_swap(a, 1), dom_swap(b, 2), dom_pairs(c, 2), dom_pairs(d, 1)]


def sent_rounds():
    me = lax.axis_index("dom")
    core, chip = lax.rem(me, CORES), lax.rem(me // CORES, 2)
    return (core, 2 + chip, 3 - chip, 1 - core)


def received_rounds():
    first, second, third, fourth = sent_rounds()
    return (1 - first, 5 - second, 5 - third, 1 - fourth)


def pack_kernel(send, feats, out0, out1, out2, out3, send_now, feats_now, sems):
    copies = [
        pltpu.make_async_copy(send, send_now, sems.at[0]),
        pltpu.make_async_copy(feats, feats_now, sems.at[1]),
    ]
    for copy in copies:
        copy.start()
    for copy in copies:
        copy.wait()
    for r, out in zip(sent_rounds(), (out0, out1, out2, out3)):
        for s in range(NB):
            out[s * BS : (s + 1) * BS, :] = feats_now[rows(send_now[0, s, r]), :]


def before_kernel(
    neighbors,
    recv,
    live,
    feats,
    self_w,
    tiles,
    edge_tiles,
    local,
    edge,
    local_sum,
    degree,
    own_pre,
    turned,
    neighbors_now,
    recv_now,
    live_now,
    feats_now,
    self_w_now,
    tiles_now,
    edge_tiles_now,
    sems,
):
    pairs = (
        (neighbors, neighbors_now),
        (recv, recv_now),
        (live, live_now),
        (tiles, tiles_now),
        (edge_tiles, edge_tiles_now),
        (feats, feats_now),
        (self_w, self_w_now),
    )
    copies = [pltpu.make_async_copy(a, b, sems.at[i]) for i, (a, b) in enumerate(pairs)]
    for copy in copies:
        copy.start()
    local[...] = jnp.zeros_like(local)
    edge[...] = jnp.zeros_like(edge)
    for copy in copies:
        copy.wait()
    for b in range(BLK):
        for k in range(K_IN):
            cols = rows(neighbors_now[0, b, k])
            here = slice(b * BS, (b + 1) * BS)
            local[here, cols] = local[here, cols] + tiles_now[0, b, k]
    for i, r in enumerate(received_rounds()):
        for s in range(NB):
            slot = i * NB + s

            @pl.when(s < live_now[0, r])
            def _():
                edge[rows(recv_now[0, s, r]), slot * BS : (slot + 1) * BS] = edge_tiles_now[0, r, s]

    mine = feats_now[...]
    own_pre[...] = dot(mine, self_w_now[...])
    turned[...] = mine.T
    whole = local[...]
    local_sum[...] = dot(whole, mine)
    ones = jnp.ones((BS * BLK, BS), BF16)
    edge_ones = jnp.ones((BS * NB * ROUNDS, BS), BF16)
    degree[...] = dot(whole, ones) + dot(edge[...], edge_ones)


def middle_kernel(
    edge,
    got0,
    got1,
    got2,
    got3,
    local_sum,
    degree,
    own_pre,
    neigh_w,
    cot,
    turned,
    activated,
    low_out,
    spread_out,
    keep,
    give,
):
    core = lax.rem(lax.axis_index("dom"), CORES)
    width = NB * BS
    total = local_sum[...]
    for r, got in enumerate((got0, got1, got2, got3)):
        total = total + dot(edge[:, r * width : (r + 1) * width], got[...])
    inverse = 1.0 / degree[...]
    mean = total * jnp.concatenate([inverse] * (total.shape[1] // BS), axis=1)
    mean_high = mean.astype(BF16)
    mean_rest = (mean - mean_high.astype(F32)).astype(BF16)
    weights = neigh_w[...]
    pre = own_pre[...] + dot(mean_high, weights) + dot(mean_rest, weights)
    sig = jax.nn.sigmoid(pre)
    activated[...] = (pre * sig).astype(BF16)
    grad = cot[...].astype(F32) * sig * (1.0 + pre * (1.0 - sig))
    low = grad.astype(BF16)
    low_out[...] = low
    spread = (grad * jnp.concatenate([inverse] * (grad.shape[1] // BS), axis=1)).astype(BF16)
    spread_out[...] = spread
    of_self = dot(turned[...], low)
    of_neigh = dot(mean_high, low, ((0,), (0,)))

    @pl.when(core == 0)
    def _():
        keep[...] = of_self
        give[...] = of_neigh.astype(BF16)

    @pl.when(core == 1)
    def _():
        keep[...] = of_neigh
        give[...] = of_self.astype(BF16)


def piece_at(i):
    return (i % 16) * PIECE[0], (i // 16) * PIECE[1]


def cut_kernel(keep, got, out):
    total = keep[...] + got[...].astype(F32)
    for i in range(CHIPS):
        at, lane = piece_at(i)
        out[i] = total[at : at + PIECE[0], lane : lane + PIECE[1]].astype(BF16)


def sum_kernel(got, out):
    done = jnp.sum(got[...].astype(F32), axis=0).astype(BF16)
    for i in range(CHIPS):
        out[i] = done


def last_kernel(scale, mine, other, of_self, of_neigh):
    core = lax.rem(lax.axis_index("dom"), CORES)

    def put(a, out):
        for i in range(CHIPS):
            at, lane = piece_at(i)
            out[at : at + PIECE[0], lane : lane + PIECE[1]] = a[i].astype(F32) * scale

    @pl.when(core == 0)
    def _():
        put(mine, of_self)
        put(other, of_neigh)

    @pl.when(core == 1)
    def _():
        put(other, of_self)
        put(mine, of_neigh)


def back_own_kernel(
    edge, spread, act, local, low, self_w, term0, term1, term2, term3, activated, back, part
):
    over_rows = ((0,), (0,))
    width = NB * BS
    for r, term in enumerate((term0, term1, term2, term3)):
        of_round = edge[:, r * width : (r + 1) * width]
        term[...] = dot(of_round, spread[...], over_rows).astype(BF16)
    activated[...] = act[...]
    back[...] = dot(local[...], spread[...], over_rows)
    part[...] = dot(self_w[...], low[...], ((1,), (1,)))


def back_kernel(send, start, part, got0, got1, got2, got3, neigh_w, own, give1, give2, give3, back):
    back[...] = start[...]
    for r, got in zip(sent_rounds(), (got0, got1, got2, got3)):
        for s in range(NB):
            at = rows(send[0, s, r])
            back[at, :] = back[at, :] + got[s * BS : (s + 1) * BS, :].astype(F32)
    back_low = back[...].astype(BF16)
    y = lax.axis_index("hid")
    size = own.shape[0]
    for k in range(HID):
        at = rows(jnp.bitwise_xor(y, k), size)
        total = part[at, :] + dot(neigh_w[at, :], back_low, ((1,), (1,)))
        if k == 0:
            own[...] = total
        else:
            (give1, give2, give3)[k - 1][...] = total.astype(BF16)


def on_device(
    features,
    self_weight,
    neigh_weight,
    cotangent,
    neighbor_blocks,
    local_tiles,
    send_blocks,
    recv_blocks,
    live_slots,
    boundary_tiles,
):
    n, width = features.shape
    hidden = self_weight.shape[1]
    slots = ROUNDS * NB * BS
    send_blocks = jnp.swapaxes(send_blocks, 1, 2)
    recv_blocks = jnp.swapaxes(recv_blocks, 1, 2)
    packed = call(
        pack_kernel,
        [((NB * BS, width), BF16)] * ROUNDS,
        [HBM] * 2,
        nbytes=2_000_000,
        scratch=[pltpu.SMEM((1, NB, ROUNDS), jnp.int32), pltpu.VMEM((n, width), BF16), DMA((2,))],
    )(in_hbm(send_blocks), in_hbm(features))
    received = swaps(packed)
    local, edge, local_sum, degree, own_pre, turned = call(
        before_kernel,
        [
            ((n, n), BF16),
            ((n, slots), BF16),
            ((n, width), F32),
            ((n, BS), F32),
            ((n, hidden), F32),
            ((width, n), BF16),
        ],
        [HBM] * 7,
        flops=1_000_000_000,
        nbytes=6_000_000,
        scratch=[
            pltpu.SMEM((1, BLK, K_IN), jnp.int32),
            pltpu.SMEM((1, NB, ROUNDS), jnp.int32),
            pltpu.SMEM((1, ROUNDS), jnp.int32),
            pltpu.VMEM((n, width), BF16),
            pltpu.VMEM((width, hidden), BF16),
            pltpu.VMEM((1, BLK, K_IN, BS, BS), BF16),
            pltpu.VMEM((1, ROUNDS, NB, BS, BS), BF16),
            DMA((7,)),
        ],
    )(
        in_hbm(neighbor_blocks),
        in_hbm(recv_blocks),
        in_hbm(live_slots),
        in_hbm(features),
        in_hbm(self_weight),
        in_hbm(local_tiles),
        in_hbm(boundary_tiles),
    )
    act, low, spread, keep, give = call(
        middle_kernel,
        [((n, hidden), BF16)] * 3 + [((width, hidden), F32), ((width, hidden), BF16)],
        [VMEM] * 11,
        flops=1_600_000_000,
        nbytes=8_000_000,
        limit=32,
    )(edge, *received, local_sum, degree, own_pre, neigh_weight, cotangent, turned)

    got = dom_swap(give, 1)
    *terms, activated, back, in_part = call(
        back_own_kernel,
        [((NB * BS, hidden), BF16)] * ROUNDS
        + [((n, hidden), BF16), ((n, hidden), F32), ((width, n), F32)],
        [VMEM] * 6,
        flops=600_000_000,
        nbytes=3_000_000,
    )(edge, spread, act, local, low, self_weight)
    got, back, *terms = lax.optimization_barrier((got, back, *terms))
    returned = swaps(terms)
    pieces = (CHIPS,) + PIECE
    (cut,) = call(cut_kernel, [(pieces, BF16)], [VMEM] * 2, nbytes=1_500_000)(keep, got)
    (summed,) = call(sum_kernel, [(pieces, BF16)], [VMEM], nbytes=700_000)(exchange(cut))
    summed, back, *returned = lax.optimization_barrier((summed, back, *returned))
    shape = (width // HID, n)
    in_own, *in_gives = call(
        back_kernel,
        [(shape, F32)] + [(shape, BF16)] * (HID - 1),
        [pl.BlockSpec(memory_space=pltpu.SMEM)] + [VMEM] * 7,
        flops=300_000_000,
        nbytes=3_000_000,
        scratch=[pltpu.VMEM((n, hidden), F32)],
    )(send_blocks, back, in_part, *returned, neigh_weight)
    in_parts = [hid_swap(in_gives[k - 1], k) for k in range(1, HID)]
    mine = exchange(summed)
    other = dom_swap(mine, 1)
    scale = 1.0 / math.sqrt(n * lax.axis_size("dom"))
    grad_self, grad_neigh = call(
        functools.partial(last_kernel, scale),
        [((width, hidden), F32)] * 2,
        [VMEM] * 2,
        nbytes=2_000_000,
    )(mine, other)
    grad_input = in_own
    for part in in_parts:
        grad_input = grad_input + part.astype(F32)
    return activated, grad_self, grad_neigh, grad_input.astype(BF16).T


def solution(mesh):
    return jax.shard_map(
        on_device,
        mesh=mesh,
        in_specs=(
            P("dom", None),
            P(None, "hid"),
            P(None, "hid"),
            P("dom", "hid"),
            P("dom", None, None),
            P("dom", None, None, None, None),
            P("dom", None, None),
            P("dom", None, None),
            P("dom", None),
            P("dom", None, None, None, None),
        ),
        out_specs=(P("dom", "hid"), P(None, "hid"), P(None, "hid"), P("dom", "hid")),
        check_vma=False,
    )
```

```python
import functools
import math

import jax
import jax.numpy as jnp
from jax import lax
from jax.experimental import pallas as pl
from jax.experimental.pallas import tpu as pltpu
from jax.sharding import PartitionSpec as P

BS = 128
BLK = 4
K_IN = 8
ROUNDS = 4
NB = 2
CORES = 2
Z = 8
X = 4
HID = 4
CHIPS = X * Z
PIECE = (40, 128)
COVER_FLOPS = 60_000_000_000
BF16 = jnp.bfloat16
F32 = jnp.float32

VMEM = pl.BlockSpec(memory_space=pltpu.VMEM)
HBM = pl.BlockSpec(memory_space=pltpu.MemorySpace.HBM)
DMA = pltpu.SemaphoreType.DMA


def dot(a, b, dims=((1,), (0,))):
    return lax.dot_general(a, b, (dims, ((), ())), preferred_element_type=F32)


def call(kernel, outs, specs, flops=0, nbytes=0, limit=12, scratch=()):
    return pl.pallas_call(
        kernel,
        out_shape=[jax.ShapeDtypeStruct(shape, dtype) for shape, dtype in outs],
        in_specs=specs,
        out_specs=[VMEM] * len(outs),
        scratch_shapes=list(scratch),
        compiler_params=pltpu.CompilerParams(vmem_limit_bytes=limit * 1024 * 1024),
        cost_estimate=pl.CostEstimate(flops=flops, bytes_accessed=nbytes, transcendentals=0),
    )


def dom_swap(array, mask):
    count = lax.axis_size("dom")
    return lax.ppermute(array, "dom", [(i, i ^ mask) for i in range(count)])


def dom_pairs(array, step):
    count = lax.axis_size("dom")
    odd = [i for i in range(count) if (i // step) % 2]
    pairs = [(i, (i + step) % count) for i in odd]
    return lax.ppermute(array, "dom", pairs + [(j, i) for i, j in pairs])


def hid_swap(array, mask):
    return lax.ppermute(array, "hid", [(i, i ^ mask) for i in range(HID)])


def exchange(array):
    groups = [[CORES * chip + core for chip in range(CHIPS)] for core in range(CORES)]
    return lax.all_to_all(array, "dom", 0, 0, axis_index_groups=groups)


def in_hbm(array):
    return pltpu.with_memory_space_constraint(array, pltpu.MemorySpace.HBM)


def rows(block, size=BS):
    return pl.ds(pl.multiple_of(block * size, size), size)


def swaps(arrays):
    a, b, c, d = arrays
    return [dom_pairs(a, 2), dom_pairs(b, 1), dom_swap(c, 2), dom_swap(d, 1)]


def sent_rounds():
    me = lax.axis_index("dom")
    core, chip = lax.rem(me, CORES), lax.rem(me // CORES, 2)
    return (3 - chip, 1 - core, 2 + chip, core)


def received_rounds():
    first, second, third, fourth = sent_rounds()
    return (5 - first, 1 - second, 5 - third, 1 - fourth)


def pack_kernel(send, feats, out0, out1, out2, out3, send_now, feats_now, sems):
    copies = [
        pltpu.make_async_copy(send, send_now, sems.at[0]),
        pltpu.make_async_copy(feats, feats_now, sems.at[1]),
    ]
    for copy in copies:
        copy.start()
    for copy in copies:
        copy.wait()
    for r, out in zip(sent_rounds(), (out0, out1, out2, out3)):
        for s in range(NB):
            out[s * BS : (s + 1) * BS, :] = feats_now[rows(send_now[0, s, r]), :]


def before_kernel(
    neighbors,
    recv,
    live,
    feats,
    self_w,
    tiles,
    edge_tiles,
    local,
    edge,
    local_sum,
    degree,
    own_pre,
    turned,
    neighbors_now,
    recv_now,
    live_now,
    feats_now,
    self_w_now,
    tiles_now,
    edge_tiles_now,
    sems,
):
    pairs = (
        (neighbors, neighbors_now),
        (recv, recv_now),
        (live, live_now),
        (tiles, tiles_now),
        (edge_tiles, edge_tiles_now),
        (feats, feats_now),
        (self_w, self_w_now),
    )
    copies = [pltpu.make_async_copy(a, b, sems.at[i]) for i, (a, b) in enumerate(pairs)]
    for copy in copies:
        copy.start()
    local[...] = jnp.zeros_like(local)
    edge[...] = jnp.zeros_like(edge)
    for copy in copies:
        copy.wait()
    for b in range(BLK):
        for k in range(K_IN):
            cols = rows(neighbors_now[0, b, k])
            here = slice(b * BS, (b + 1) * BS)
            local[here, cols] = local[here, cols] + tiles_now[0, b, k]
    for i, r in enumerate(received_rounds()):
        for s in range(NB):
            slot = i * NB + s

            @pl.when(s < live_now[0, r])
            def _():
                edge[rows(recv_now[0, s, r]), slot * BS : (slot + 1) * BS] = edge_tiles_now[0, r, s]

    mine = feats_now[...]
    own_pre[...] = dot(mine, self_w_now[...])
    turned[...] = mine.T
    whole = local[...]
    local_sum[...] = dot(whole, mine)
    ones = jnp.ones((BS * BLK, BS), BF16)
    edge_ones = jnp.ones((BS * NB * ROUNDS, BS), BF16)
    degree[...] = dot(whole, ones) + dot(edge[...], edge_ones)


def middle_kernel(
    edge,
    got0,
    got1,
    got2,
    got3,
    local_sum,
    degree,
    own_pre,
    neigh_w,
    cot,
    turned,
    activated,
    low_out,
    spread_out,
    keep,
    give,
):
    core = lax.rem(lax.axis_index("dom"), CORES)
    width = NB * BS
    total = local_sum[...]
    for r, got in enumerate((got0, got1, got2, got3)):
        total = total + dot(edge[:, r * width : (r + 1) * width], got[...])
    inverse = 1.0 / degree[...]
    mean = total * jnp.concatenate([inverse] * (total.shape[1] // BS), axis=1)
    mean_high = mean.astype(BF16)
    mean_rest = (mean - mean_high.astype(F32)).astype(BF16)
    weights = neigh_w[...]
    pre = own_pre[...] + dot(mean_high, weights) + dot(mean_rest, weights)
    sig = jax.nn.sigmoid(pre)
    activated[...] = (pre * sig).astype(BF16)
    grad = cot[...].astype(F32) * sig * (1.0 + pre * (1.0 - sig))
    low = grad.astype(BF16)
    low_out[...] = low
    spread = (grad * jnp.concatenate([inverse] * (grad.shape[1] // BS), axis=1)).astype(BF16)
    spread_out[...] = spread
    of_self = dot(turned[...], low)
    of_neigh = dot(mean_high, low, ((0,), (0,)))

    @pl.when(core == 0)
    def _():
        keep[...] = of_self
        give[...] = of_neigh.astype(BF16)

    @pl.when(core == 1)
    def _():
        keep[...] = of_neigh
        give[...] = of_self.astype(BF16)


def piece_at(i):
    return (i % 16) * PIECE[0], (i // 16) * PIECE[1]


def cut_kernel(keep, got, out):
    total = keep[...] + got[...].astype(F32)
    for i in range(CHIPS):
        at, lane = piece_at(i)
        out[i] = total[at : at + PIECE[0], lane : lane + PIECE[1]].astype(BF16)


def sum_kernel(got, out):
    done = jnp.sum(got[...].astype(F32), axis=0).astype(BF16)
    for i in range(CHIPS):
        out[i] = done


def last_kernel(scale, mine, other, of_self, of_neigh):
    core = lax.rem(lax.axis_index("dom"), CORES)

    def put(a, out):
        for i in range(CHIPS):
            at, lane = piece_at(i)
            out[at : at + PIECE[0], lane : lane + PIECE[1]] = a[i].astype(F32) * scale

    @pl.when(core == 0)
    def _():
        put(mine, of_self)
        put(other, of_neigh)

    @pl.when(core == 1)
    def _():
        put(other, of_self)
        put(mine, of_neigh)


def back_own_kernel(
    send,
    edge,
    spread,
    act,
    local,
    low,
    self_w,
    neigh_w,
    term0,
    term1,
    term2,
    term3,
    activated,
    back,
    part,
    neigh_w_out,
    place,
    send_now,
    sem,
):
    copy = pltpu.make_async_copy(send, send_now, sem.at[0])
    copy.start()
    over_rows = ((0,), (0,))
    width = NB * BS
    for r, term in enumerate((term0, term1, term2, term3)):
        of_round = edge[:, r * width : (r + 1) * width]
        term[...] = dot(of_round, spread[...], over_rows).astype(BF16)
    activated[...] = act[...]
    back[...] = dot(local[...], spread[...], over_rows)
    part[...] = dot(self_w[...], low[...], ((1,), (1,)))
    neigh_w_out[...] = neigh_w[...]
    copy.wait()
    for i, r in enumerate(sent_rounds()):
        for s in range(NB):
            for b in range(BLK):
                at = (i * NB + s) * BLK + b
                hit = jnp.where(send_now[0, s, r] == b, 1.0, 0.0)
                place[at : at + 1, :] = jnp.full((1, BS), hit, F32)


def hid_part(k, size, part, neigh_w, back):
    at = rows(jnp.bitwise_xor(lax.axis_index("hid"), k), size)
    return part[at, :] + dot(neigh_w[at, :], back, ((1,), (1,)))


def back_kernel(
    place, start, part, got0, got1, got2, got3, neigh_w, own, far, give1, give3, got_now, sems
):
    size, hidden = own.shape[0], start.shape[1]
    copies = [
        pltpu.make_async_copy(got, got_now.at[i], sems.at[i])
        for i, got in enumerate((got0, got1, got2, got3))
    ]
    for copy in copies:
        copy.start()
    for copy in copies:
        copy.wait()
    blocks = []
    for b in range(BLK):
        total = start[b * BS : (b + 1) * BS, :]
        for i in range(ROUNDS):
            for s in range(NB):
                at = (i * NB + s) * BLK + b
                hit = jnp.concatenate([place[at : at + 1, :]] * (hidden // BS), axis=1)
                total = total + hit * got_now[i, s * BS : (s + 1) * BS, :].astype(F32)
        blocks.append(total.astype(BF16))
    back = jnp.concatenate(blocks, axis=0)
    far[...] = hid_part(2, size, part, neigh_w, back).astype(BF16)
    give1[...] = hid_part(1, size, part, neigh_w, back).astype(BF16)
    give3[...] = hid_part(3, size, part, neigh_w, back).astype(BF16)
    own[...] = hid_part(0, size, part, neigh_w, back)


def on_device(
    features,
    self_weight,
    neigh_weight,
    cotangent,
    neighbor_blocks,
    local_tiles,
    send_blocks,
    recv_blocks,
    live_slots,
    boundary_tiles,
):
    n, width = features.shape
    hidden = self_weight.shape[1]
    slots = ROUNDS * NB * BS
    send_blocks = jnp.swapaxes(send_blocks, 1, 2)
    recv_blocks = jnp.swapaxes(recv_blocks, 1, 2)
    packed = call(
        pack_kernel,
        [((NB * BS, width), BF16)] * ROUNDS,
        [HBM] * 2,
        nbytes=2_000_000,
        scratch=[pltpu.SMEM((1, NB, ROUNDS), jnp.int32), pltpu.VMEM((n, width), BF16), DMA((2,))],
    )(in_hbm(send_blocks), in_hbm(features))
    received = swaps(packed)
    local, edge, local_sum, degree, own_pre, turned = call(
        before_kernel,
        [
            ((n, n), BF16),
            ((n, slots), BF16),
            ((n, width), F32),
            ((n, BS), F32),
            ((n, hidden), F32),
            ((width, n), BF16),
        ],
        [HBM] * 7,
        flops=1_000_000_000,
        nbytes=6_000_000,
        scratch=[
            pltpu.SMEM((1, BLK, K_IN), jnp.int32),
            pltpu.SMEM((1, NB, ROUNDS), jnp.int32),
            pltpu.SMEM((1, ROUNDS), jnp.int32),
            pltpu.VMEM((n, width), BF16),
            pltpu.VMEM((width, hidden), BF16),
            pltpu.VMEM((1, BLK, K_IN, BS, BS), BF16),
            pltpu.VMEM((1, ROUNDS, NB, BS, BS), BF16),
            DMA((7,)),
        ],
    )(
        in_hbm(neighbor_blocks),
        in_hbm(recv_blocks),
        in_hbm(live_slots),
        in_hbm(features),
        in_hbm(self_weight),
        in_hbm(local_tiles),
        in_hbm(boundary_tiles),
    )
    act, low, spread, keep, give = call(
        middle_kernel,
        [((n, hidden), BF16)] * 3 + [((width, hidden), F32), ((width, hidden), BF16)],
        [VMEM] * 11,
        flops=1_600_000_000,
        nbytes=8_000_000,
        limit=16,
    )(edge, *received, local_sum, degree, own_pre, neigh_weight, cotangent, turned)

    got = dom_swap(give, 1)
    *terms, activated, back, in_part, neigh_now, place = call(
        back_own_kernel,
        [((NB * BS, hidden), BF16)] * ROUNDS
        + [((n, hidden), BF16), ((n, hidden), F32), ((width, n), F32), ((width, hidden), BF16)]
        + [((ROUNDS * NB * BLK, BS), F32)],
        [HBM] + [VMEM] * 7,
        flops=600_000_000,
        nbytes=3_000_000,
        scratch=[pltpu.SMEM((1, NB, ROUNDS), jnp.int32), DMA((1,))],
    )(in_hbm(send_blocks), edge, spread, act, local, low, self_weight, neigh_weight)
    got, back, *terms = lax.optimization_barrier((got, back, *terms))
    returned = swaps(terms)
    pieces = (CHIPS,) + PIECE
    (cut,) = call(cut_kernel, [(pieces, BF16)], [VMEM] * 2, nbytes=1_500_000)(keep, got)
    (summed,) = call(sum_kernel, [(pieces, BF16)], [VMEM], nbytes=700_000)(exchange(cut))
    summed, back = lax.optimization_barrier((summed, back))
    shape = (width // HID, n)
    in_own, in_far, in_first, in_third = call(
        back_kernel,
        [(shape, F32)] + [(shape, BF16)] * 3,
        [VMEM] * 3 + [HBM] * 4 + [VMEM],
        flops=COVER_FLOPS,
        nbytes=3_000_000,
        scratch=[pltpu.VMEM((ROUNDS, NB * BS, hidden), BF16), DMA((ROUNDS,))],
    )(place, back, in_part, *[in_hbm(a) for a in returned], neigh_now)
    in_parts = [hid_swap(in_far, 2), hid_swap(in_first, 1), hid_swap(in_third, 3)]
    mine = exchange(summed)
    other = dom_swap(mine, 1)
    scale = 1.0 / math.sqrt(n * lax.axis_size("dom"))
    grad_self, grad_neigh = call(
        functools.partial(last_kernel, scale),
        [((width, hidden), F32)] * 2,
        [VMEM] * 2,
        nbytes=2_000_000,
    )(mine, other)
    grad_self, grad_input = lax.optimization_barrier((grad_self, in_own))
    for part in in_parts:
        grad_input = grad_input + part.astype(F32)
    return activated, grad_self, grad_neigh, grad_input.astype(BF16).T


def solution(mesh):
    return jax.shard_map(
        on_device,
        mesh=mesh,
        in_specs=(
            P("dom", None),
            P(None, "hid"),
            P(None, "hid"),
            P("dom", "hid"),
            P("dom", None, None),
            P("dom", None, None, None, None),
            P("dom", None, None),
            P("dom", None, None),
            P("dom", None),
            P("dom", None, None, None, None),
        ),
        out_specs=(P("dom", "hid"), P(None, "hid"), P(None, "hid"), P("dom", "hid")),
        check_vma=False,
    )
```

```python
import functools
import math

import jax
import jax.numpy as jnp
from jax import lax
from jax.experimental import pallas as pl
from jax.experimental.pallas import tpu as pltpu
from jax.sharding import PartitionSpec as P

BS = 128
BLK = 4
K_IN = 8
ROUNDS = 4
NB = 2
CORES = 2
Z = 8
X = 4
HID = 4
CHIPS = X * Z
PIECE = (40, 128)
COVER_FLOPS = 60_000_000_000
BF16 = jnp.bfloat16
F32 = jnp.float32

VMEM = pl.BlockSpec(memory_space=pltpu.VMEM)
HBM = pl.BlockSpec(memory_space=pltpu.MemorySpace.HBM)
DMA = pltpu.SemaphoreType.DMA


def dot(a, b, dims=((1,), (0,))):
    return lax.dot_general(a, b, (dims, ((), ())), preferred_element_type=F32)


def call(kernel, outs, specs, flops=0, nbytes=0, limit=12, scratch=()):
    return pl.pallas_call(
        kernel,
        out_shape=[jax.ShapeDtypeStruct(shape, dtype) for shape, dtype in outs],
        in_specs=specs,
        out_specs=[VMEM] * len(outs),
        scratch_shapes=list(scratch),
        compiler_params=pltpu.CompilerParams(vmem_limit_bytes=limit * 1024 * 1024),
        cost_estimate=pl.CostEstimate(flops=flops, bytes_accessed=nbytes, transcendentals=0),
    )


def dom_swap(array, mask):
    count = lax.axis_size("dom")
    return lax.ppermute(array, "dom", [(i, i ^ mask) for i in range(count)])


def dom_pairs(array, step):
    count = lax.axis_size("dom")
    odd = [i for i in range(count) if (i // step) % 2]
    pairs = [(i, (i + step) % count) for i in odd]
    return lax.ppermute(array, "dom", pairs + [(j, i) for i, j in pairs])


def hid_swap(array, mask):
    return lax.ppermute(array, "hid", [(i, i ^ mask) for i in range(HID)])


def exchange(array):
    groups = [[CORES * chip + core for chip in range(CHIPS)] for core in range(CORES)]
    return lax.all_to_all(array, "dom", 0, 0, axis_index_groups=groups)


def in_hbm(array):
    return pltpu.with_memory_space_constraint(array, pltpu.MemorySpace.HBM)


def rows(block, size=BS):
    return pl.ds(pl.multiple_of(block * size, size), size)


def swaps(arrays):
    a, b, c, d = arrays
    return [dom_swap(a, 2), dom_pairs(b, 1), dom_pairs(c, 2), dom_swap(d, 1)]


def sent_rounds():
    me = lax.axis_index("dom")
    core, chip = lax.rem(me, CORES), lax.rem(me // CORES, 2)
    return (2 + chip, 1 - core, 3 - chip, core)


def received_rounds():
    first, second, third, fourth = sent_rounds()
    return (5 - first, 1 - second, 5 - third, 1 - fourth)


def pack_kernel(send, feats, out0, out1, out2, out3, send_now, feats_now, sems):
    copies = [
        pltpu.make_async_copy(send, send_now, sems.at[0]),
        pltpu.make_async_copy(feats, feats_now, sems.at[1]),
    ]
    for copy in copies:
        copy.start()
    for copy in copies:
        copy.wait()
    y, size = lax.axis_index("hid"), out1.shape[0]
    per_slot = HID // NB
    for r, out in zip(sent_rounds(), (out0, out1, out2, out3)):
        if out is out1:
            at = send_now[0, y // per_slot, r] * BS + lax.rem(y, per_slot) * size
            out[...] = feats_now[pl.ds(pl.multiple_of(at, size), size), :]
            continue
        for s in range(NB):
            out[s * BS : (s + 1) * BS, :] = feats_now[rows(send_now[0, s, r]), :]


def before_kernel(
    neighbors,
    recv,
    live,
    feats,
    self_w,
    tiles,
    edge_tiles,
    local,
    edge,
    local_sum,
    degree,
    own_pre,
    turned,
    neighbors_now,
    recv_now,
    live_now,
    feats_now,
    self_w_now,
    tiles_now,
    edge_tiles_now,
    sems,
):
    pairs = (
        (feats, feats_now),
        (self_w, self_w_now),
        (neighbors, neighbors_now),
        (recv, recv_now),
        (live, live_now),
        (tiles, tiles_now),
        (edge_tiles, edge_tiles_now),
    )
    copies = [pltpu.make_async_copy(a, b, sems.at[i]) for i, (a, b) in enumerate(pairs)]
    for copy in copies:
        copy.start()
    local[...] = jnp.zeros_like(local)
    edge[...] = jnp.zeros_like(edge)
    for copy in copies[:2]:
        copy.wait()
    mine = feats_now[...]
    own_pre[...] = dot(mine, self_w_now[...])
    turned[...] = mine.T
    for copy in copies[2:]:
        copy.wait()
    for b in range(BLK):
        for k in range(K_IN):
            cols = rows(neighbors_now[0, b, k])
            here = slice(b * BS, (b + 1) * BS)
            local[here, cols] = local[here, cols] + tiles_now[0, b, k]
    for i, r in enumerate(received_rounds()):
        for s in range(NB):
            slot = i * NB + s

            @pl.when(s < live_now[0, r])
            def _():
                edge[rows(recv_now[0, s, r]), slot * BS : (slot + 1) * BS] = edge_tiles_now[0, r, s]

    whole = local[...]
    local_sum[...] = dot(whole, mine)
    ones = jnp.ones((BS * BLK, BS), BF16)
    edge_ones = jnp.ones((BS * NB * ROUNDS, BS), BF16)
    degree[...] = dot(whole, ones) + dot(edge[...], edge_ones)


def middle_kernel(
    edge,
    got0,
    got2,
    got3,
    share0,
    share1,
    share2,
    share3,
    local_sum,
    degree,
    own_pre,
    neigh_w,
    cot,
    turned,
    activated,
    low_out,
    spread_out,
    mean_out,
    give,
    got1,
):
    size = share0.shape[0]
    for k, share in zip((0, 2, 1, 3), (share0, share1, share2, share3)):
        got1[rows(jnp.bitwise_xor(lax.axis_index("hid"), k), size), :] = share[...]
    core = lax.rem(lax.axis_index("dom"), CORES)
    width = NB * BS
    total = local_sum[...]
    for r, got in enumerate((got0, got1, got2, got3)):
        total = total + dot(edge[:, r * width : (r + 1) * width], got[...])
    inverse = 1.0 / degree[...]
    mean = total * jnp.concatenate([inverse] * (total.shape[1] // BS), axis=1)
    mean_high = mean.astype(BF16)
    mean_rest = (mean - mean_high.astype(F32)).astype(BF16)
    weights = neigh_w[...]
    pre = own_pre[...] + dot(mean_high, weights) + dot(mean_rest, weights)
    sig = jax.nn.sigmoid(pre)
    activated[...] = (pre * sig).astype(BF16)
    grad = cot[...].astype(F32) * sig * (1.0 + pre * (1.0 - sig))
    low = grad.astype(BF16)
    low_out[...] = low
    spread = (grad * jnp.concatenate([inverse] * (grad.shape[1] // BS), axis=1)).astype(BF16)
    spread_out[...] = spread
    mean_out[...] = mean_high

    @pl.when(core == 0)
    def _():
        give[...] = dot(mean_high, low, ((0,), (0,))).astype(BF16)

    @pl.when(core == 1)
    def _():
        give[...] = dot(turned[...], low).astype(BF16)


def keep_kernel(turned, mean, low, keep):
    core = lax.rem(lax.axis_index("dom"), CORES)

    @pl.when(core == 0)
    def _():
        keep[...] = dot(turned[...], low[...])

    @pl.when(core == 1)
    def _():
        keep[...] = dot(mean[...], low[...], ((0,), (0,)))


def piece_at(i):
    return (i % 16) * PIECE[0], (i // 16) * PIECE[1]


def cut_kernel(keep, got, out):
    total = keep[...] + got[...].astype(F32)
    for i in range(CHIPS):
        at, lane = piece_at(i)
        out[i] = total[at : at + PIECE[0], lane : lane + PIECE[1]].astype(BF16)


def sum_kernel(got, out):
    done = jnp.sum(got[...].astype(F32), axis=0).astype(BF16)
    for i in range(CHIPS):
        out[i] = done


def last_kernel(scale, mine, other, of_self, of_neigh):
    core = lax.rem(lax.axis_index("dom"), CORES)

    def put(a, out):
        for i in range(CHIPS):
            at, lane = piece_at(i)
            out[at : at + PIECE[0], lane : lane + PIECE[1]] = a[i].astype(F32) * scale

    @pl.when(core == 0)
    def _():
        put(mine, of_self)
        put(other, of_neigh)

    @pl.when(core == 1)
    def _():
        put(other, of_self)
        put(mine, of_neigh)


def back_own_kernel(
    send,
    edge,
    spread,
    act,
    local,
    self_w,
    neigh_w,
    term0,
    term1,
    term2,
    term3,
    activated,
    back,
    self_w_out,
    neigh_w_out,
    place,
    send_now,
    sem,
):
    copy = pltpu.make_async_copy(send, send_now, sem.at[0])
    copy.start()
    over_rows = ((0,), (0,))
    width = NB * BS
    for r, term in enumerate((term0, term1, term2, term3)):
        of_round = edge[:, r * width : (r + 1) * width]
        term[...] = dot(of_round, spread[...], over_rows).astype(BF16)
    activated[...] = act[...]
    back[...] = dot(local[...], spread[...], over_rows)
    self_w_out[...] = self_w[...]
    neigh_w_out[...] = neigh_w[...]
    copy.wait()
    for i, r in enumerate(sent_rounds()):
        for s in range(NB):
            for b in range(BLK):
                at = (i * NB + s) * BLK + b
                hit = jnp.where(send_now[0, s, r] == b, 1.0, 0.0)
                place[at : at + 1, :] = jnp.full((1, BS), hit, F32)


def hid_part(k, size, self_w, neigh_w, low, back):
    at = rows(jnp.bitwise_xor(lax.axis_index("hid"), k), size)
    over_hidden = ((1,), (1,))
    return dot(self_w[at, :], low, over_hidden) + dot(neigh_w[at, :], back, over_hidden)


def back_kernel(
    place, start, low, self_w, neigh_w, got0, got1, got2, got3, own, far, give1, give3
):
    size, hidden = own.shape[0], start.shape[1]
    blocks = []
    for b in range(BLK):
        total = start[b * BS : (b + 1) * BS, :]
        for i, got in enumerate((got0, got1, got2, got3)):
            for s in range(NB):
                at = (i * NB + s) * BLK + b
                hit = jnp.concatenate([place[at : at + 1, :]] * (hidden // BS), axis=1)
                total = total + hit * got[s * BS : (s + 1) * BS, :].astype(F32)
        blocks.append(total.astype(BF16))
    back = jnp.concatenate(blocks, axis=0)
    part = functools.partial(hid_part, size=size, self_w=self_w, neigh_w=neigh_w)
    low_now = low[...]
    far[...] = part(2, low=low_now, back=back).astype(BF16)
    give1[...] = part(1, low=low_now, back=back).astype(BF16)
    give3[...] = part(3, low=low_now, back=back).astype(BF16)
    own[...] = part(0, low=low_now, back=back)


def on_device(
    features,
    self_weight,
    neigh_weight,
    cotangent,
    neighbor_blocks,
    local_tiles,
    send_blocks,
    recv_blocks,
    live_slots,
    boundary_tiles,
):
    n, width = features.shape
    hidden = self_weight.shape[1]
    slots = ROUNDS * NB * BS
    send_blocks = jnp.swapaxes(send_blocks, 1, 2)
    recv_blocks = jnp.swapaxes(recv_blocks, 1, 2)
    packed = call(
        pack_kernel,
        [((NB * BS // HID if r == 1 else NB * BS, width), BF16) for r in range(ROUNDS)],
        [HBM] * 2,
        nbytes=2_000_000,
        scratch=[pltpu.SMEM((1, NB, ROUNDS), jnp.int32), pltpu.VMEM((n, width), BF16), DMA((2,))],
    )(in_hbm(send_blocks), in_hbm(features))
    got_c, share, got_d, got_a = swaps(packed)
    share, got_a = lax.optimization_barrier((share, got_a))
    shares = [share] + [hid_swap(share, k) for k in (2, 1, 3)]
    local, edge, local_sum, degree, own_pre, turned = call(
        before_kernel,
        [
            ((n, n), BF16),
            ((n, slots), BF16),
            ((n, width), F32),
            ((n, BS), F32),
            ((n, hidden), F32),
            ((width, n), BF16),
        ],
        [HBM] * 7,
        flops=COVER_FLOPS,
        nbytes=6_000_000,
        scratch=[
            pltpu.SMEM((1, BLK, K_IN), jnp.int32),
            pltpu.SMEM((1, NB, ROUNDS), jnp.int32),
            pltpu.SMEM((1, ROUNDS), jnp.int32),
            pltpu.VMEM((n, width), BF16),
            pltpu.VMEM((width, hidden), BF16),
            pltpu.VMEM((1, BLK, K_IN, BS, BS), BF16),
            pltpu.VMEM((1, ROUNDS, NB, BS, BS), BF16),
            DMA((7,)),
        ],
    )(
        in_hbm(neighbor_blocks),
        in_hbm(recv_blocks),
        in_hbm(live_slots),
        in_hbm(features),
        in_hbm(self_weight),
        in_hbm(local_tiles),
        in_hbm(boundary_tiles),
    )
    act, low, spread, mean, give = call(
        middle_kernel,
        [((n, hidden), BF16)] * 3 + [((n, width), BF16), ((width, hidden), BF16)],
        [VMEM] * 14,
        flops=1_600_000_000,
        nbytes=8_000_000,
        scratch=[pltpu.VMEM((NB * BS, width), BF16)],
        limit=16,
    )(edge, got_c, got_d, got_a, *shares, local_sum, degree, own_pre, neigh_weight, cotangent, turned)

    got = dom_swap(give, 1)
    (keep,) = call(
        keep_kernel, [((width, hidden), F32)], [VMEM] * 3, flops=200_000_000, nbytes=2_000_000
    )(turned, mean, low)
    got, keep = lax.optimization_barrier((got, keep))
    pieces = (CHIPS,) + PIECE
    (cut,) = call(cut_kernel, [(pieces, BF16)], [VMEM] * 2, nbytes=1_500_000)(keep, got)
    cut, spread, low = lax.optimization_barrier((cut, spread, low))
    *terms, activated, back, self_now, neigh_now, place = call(
        back_own_kernel,
        [((NB * BS, hidden), BF16)] * ROUNDS
        + [((n, hidden), BF16), ((n, hidden), F32)]
        + [((width, hidden), BF16)] * 2
        + [((ROUNDS * NB * BLK, BS), F32)],
        [HBM] + [VMEM] * 6,
        flops=600_000_000,
        nbytes=3_000_000,
        scratch=[pltpu.SMEM((1, NB, ROUNDS), jnp.int32), DMA((1,))],
    )(in_hbm(send_blocks), edge, spread, act, local, self_weight, neigh_weight)
    returned = swaps(terms)
    (summed,) = call(sum_kernel, [(pieces, BF16)], [VMEM], nbytes=700_000)(exchange(cut))
    summed, back = lax.optimization_barrier((summed, back))
    shape = (width // HID, n)
    in_own, in_far, in_first, in_third = call(
        back_kernel,
        [(shape, F32)] + [(shape, BF16)] * 3,
        [VMEM] * 9,
        flops=COVER_FLOPS,
        nbytes=3_000_000,
    )(place, back, low, self_now, neigh_now, *returned)
    in_parts = [hid_swap(in_far, 2), hid_swap(in_first, 1), hid_swap(in_third, 3)]
    mine = exchange(summed)
    other = dom_swap(mine, 1)
    scale = 1.0 / math.sqrt(n * lax.axis_size("dom"))
    grad_self, grad_neigh = call(
        functools.partial(last_kernel, scale),
        [((width, hidden), F32)] * 2,
        [VMEM] * 2,
        nbytes=2_000_000,
    )(mine, other)
    grad_input = in_own
    for part in in_parts:
        grad_input = grad_input + part.astype(F32)
    return activated, grad_self, grad_neigh, grad_input.astype(BF16).T


def solution(mesh):
    return jax.shard_map(
        on_device,
        mesh=mesh,
        in_specs=(
            P("dom", None),
            P(None, "hid"),
            P(None, "hid"),
            P("dom", "hid"),
            P("dom", None, None),
            P("dom", None, None, None, None),
            P("dom", None, None),
            P("dom", None, None),
            P("dom", None),
            P("dom", None, None, None, None),
        ),
        out_specs=(P("dom", "hid"), P(None, "hid"), P(None, "hid"), P("dom", "hid")),
        check_vma=False,
    )
```

```python
import functools
import math

import jax
import jax.numpy as jnp
from jax import lax
from jax.experimental import pallas as pl
from jax.experimental.pallas import tpu as pltpu
from jax.sharding import PartitionSpec as P

BS = 128
BLK = 4
K_IN = 8
ROUNDS = 4
NB = 2
CORES = 2
Z = 8
X = 4
HID = 4
CHIPS = X * Z
PIECE = (40, 128)
COVER_FLOPS = 60_000_000_000
BF16 = jnp.bfloat16
F32 = jnp.float32

VMEM = pl.BlockSpec(memory_space=pltpu.VMEM)
HBM = pl.BlockSpec(memory_space=pltpu.MemorySpace.HBM)
DMA = pltpu.SemaphoreType.DMA


def dot(a, b, dims=((1,), (0,))):
    return lax.dot_general(a, b, (dims, ((), ())), preferred_element_type=F32)


def call(kernel, outs, specs, flops=0, nbytes=0, limit=12, scratch=()):
    return pl.pallas_call(
        kernel,
        out_shape=[jax.ShapeDtypeStruct(shape, dtype) for shape, dtype in outs],
        in_specs=specs,
        out_specs=[VMEM] * len(outs),
        scratch_shapes=list(scratch),
        compiler_params=pltpu.CompilerParams(vmem_limit_bytes=limit * 1024 * 1024),
        cost_estimate=pl.CostEstimate(flops=flops, bytes_accessed=nbytes, transcendentals=0),
    )


def dom_swap(array, mask):
    count = lax.axis_size("dom")
    return lax.ppermute(array, "dom", [(i, i ^ mask) for i in range(count)])


def dom_pairs(array, step):
    count = lax.axis_size("dom")
    odd = [i for i in range(count) if (i // step) % 2]
    pairs = [(i, (i + step) % count) for i in odd]
    return lax.ppermute(array, "dom", pairs + [(j, i) for i, j in pairs])


def hid_swap(array, mask):
    return lax.ppermute(array, "hid", [(i, i ^ mask) for i in range(HID)])


def exchange(array):
    chips = list(reversed(range(CHIPS)))
    groups = [[CORES * chip + core for chip in chips] for core in range(CORES)]
    return lax.all_to_all(array, "dom", 0, 0, axis_index_groups=groups)


def in_hbm(array):
    return pltpu.with_memory_space_constraint(array, pltpu.MemorySpace.HBM)


def rows(block, size=BS):
    return pl.ds(pl.multiple_of(block * size, size), size)


def swaps(arrays):
    a, b, c, d = arrays
    return [dom_pairs(a, 2), dom_pairs(b, 1), dom_swap(c, 2), dom_swap(d, 1)]


def sent_rounds():
    me = lax.axis_index("dom")
    core, chip = lax.rem(me, CORES), lax.rem(me // CORES, 2)
    return (3 - chip, 1 - core, 2 + chip, core)


def received_rounds():
    first, second, third, fourth = sent_rounds()
    return (5 - first, 1 - second, 5 - third, 1 - fourth)


def pack_kernel(send, feats, out0, out1, out2, out3, feats_now, send_now, sems):
    copies = [
        pltpu.make_async_copy(send, send_now, sems.at[0]),
        pltpu.make_async_copy(feats, feats_now, sems.at[1]),
    ]
    for copy in copies:
        copy.start()
    for copy in copies:
        copy.wait()
    y, size = lax.axis_index("hid"), out1.shape[0]
    per_slot = HID // NB
    for r, out in zip(sent_rounds(), (out0, out1, out2, out3)):
        if out is out1:
            at = send_now[0, y // per_slot, r] * BS + lax.rem(y, per_slot) * size
            out[...] = feats_now[pl.ds(pl.multiple_of(at, size), size), :]
            continue
        for s in range(NB):
            out[s * BS : (s + 1) * BS, :] = feats_now[rows(send_now[0, s, r]), :]


def turn_kernel(feats, turned):
    turned[...] = feats[...].T


def before_kernel(
    neighbors,
    recv,
    live,
    self_w,
    tiles,
    edge_tiles,
    feats,
    got,
    local,
    edge,
    local_sum,
    inverse,
    own_pre,
    neighbors_now,
    recv_now,
    live_now,
    self_w_now,
    tiles_now,
    edge_tiles_now,
    sems,
):
    pairs = (
        (self_w, self_w_now),
        (neighbors, neighbors_now),
        (recv, recv_now),
        (live, live_now),
        (tiles, tiles_now),
        (edge_tiles, edge_tiles_now),
    )
    copies = [pltpu.make_async_copy(a, b, sems.at[i]) for i, (a, b) in enumerate(pairs)]
    for copy in copies:
        copy.start()
    local[...] = jnp.zeros_like(local)
    edge[...] = jnp.zeros_like(edge)
    copies[0].wait()
    mine = feats[...]
    own_pre[...] = dot(mine, self_w_now[...])
    for copy in copies[1:]:
        copy.wait()
    for b in range(BLK):
        for k in range(K_IN):
            cols = rows(neighbors_now[0, b, k])
            here = slice(b * BS, (b + 1) * BS)
            local[here, cols] = local[here, cols] + tiles_now[0, b, k]
    for i, r in enumerate(received_rounds()):
        for s in range(NB):
            slot = i * NB + s

            @pl.when(s < live_now[0, r])
            def _():
                edge[rows(recv_now[0, s, r]), slot * BS : (slot + 1) * BS] = edge_tiles_now[0, r, s]

    whole = local[...]
    of_pair = (ROUNDS - 1) * NB * BS
    local_sum[...] = dot(whole, mine) + dot(edge[:, of_pair:], got[...])
    ones = jnp.ones((BS * BLK, BS), BF16)
    edge_ones = jnp.ones((BS * NB * ROUNDS, BS), BF16)
    inverse[...] = 1.0 / (dot(whole, ones) + dot(edge[...], edge_ones))


def middle_kernel(
    edge,
    got0,
    got2,
    share0,
    share1,
    share2,
    share3,
    local_sum,
    inverse_in,
    own_pre,
    neigh_w,
    cot,
    turned,
    activated,
    low_out,
    spread_out,
    mean_out,
    give,
    got1,
):
    size = share0.shape[0]
    for k, share in zip((0, 3, 1, 2), (share0, share1, share2, share3)):
        got1[rows(jnp.bitwise_xor(lax.axis_index("hid"), k), size), :] = share[...]
    core = lax.rem(lax.axis_index("dom"), CORES)
    width = NB * BS
    total = local_sum[...]
    for r, got in enumerate((got0, got1, got2)):
        total = total + dot(edge[:, r * width : (r + 1) * width], got[...])
    inverse = inverse_in[...]
    mean = total * jnp.concatenate([inverse] * (total.shape[1] // BS), axis=1)
    mean_high = mean.astype(BF16)
    mean_rest = (mean - mean_high.astype(F32)).astype(BF16)
    weights = neigh_w[...]
    pre = own_pre[...] + dot(mean_high, weights) + dot(mean_rest, weights)
    sig = jax.nn.sigmoid(pre)
    activated[...] = (pre * sig).astype(BF16)
    grad = cot[...].astype(F32) * sig * (1.0 + pre * (1.0 - sig))
    low = grad.astype(BF16)
    low_out[...] = low
    spread = (grad * jnp.concatenate([inverse] * (grad.shape[1] // BS), axis=1)).astype(BF16)
    spread_out[...] = spread
    mean_out[...] = mean_high

    @pl.when(core == 0)
    def _():
        give[...] = dot(mean_high, low, ((0,), (0,))).astype(BF16)

    @pl.when(core == 1)
    def _():
        give[...] = dot(turned[...], low).astype(BF16)


def keep_kernel(turned, mean, low, keep):
    core = lax.rem(lax.axis_index("dom"), CORES)

    @pl.when(core == 0)
    def _():
        keep[...] = dot(turned[...], low[...])

    @pl.when(core == 1)
    def _():
        keep[...] = dot(mean[...], low[...], ((0,), (0,)))


def piece_at(i):
    return (i % 16) * PIECE[0], (i // 16) * PIECE[1]


def cut_kernel(keep, got, out):
    total = keep[...] + got[...].astype(F32)
    for i in range(CHIPS):
        at, lane = piece_at(i)
        out[i] = total[at : at + PIECE[0], lane : lane + PIECE[1]].astype(BF16)


def sum_kernel(got, out):
    done = jnp.sum(got[...].astype(F32), axis=0).astype(BF16)
    for i in range(CHIPS):
        out[i] = done


def last_kernel(scale, mine, other, of_self, of_neigh):
    core = lax.rem(lax.axis_index("dom"), CORES)

    def put(a, out):
        for i in range(CHIPS):
            at, lane = piece_at(i)
            out[at : at + PIECE[0], lane : lane + PIECE[1]] = a[i].astype(F32) * scale

    @pl.when(core == 0)
    def _():
        put(mine, of_self)
        put(other, of_neigh)

    @pl.when(core == 1)
    def _():
        put(other, of_self)
        put(mine, of_neigh)


def back_own_kernel(
    send,
    edge,
    spread,
    act,
    local,
    self_w,
    neigh_w,
    term0,
    term1,
    term2,
    term3,
    activated,
    back,
    self_w_out,
    neigh_w_out,
    place,
    send_now,
    sem,
):
    copy = pltpu.make_async_copy(send, send_now, sem.at[0])
    copy.start()
    over_rows = ((0,), (0,))
    width = NB * BS
    for r, term in enumerate((term0, term1, term2, term3)):
        of_round = edge[:, r * width : (r + 1) * width]
        term[...] = dot(of_round, spread[...], over_rows).astype(BF16)
    activated[...] = act[...]
    back[...] = dot(local[...], spread[...], over_rows)
    self_w_out[...] = self_w[...]
    neigh_w_out[...] = neigh_w[...]
    copy.wait()
    for i, r in enumerate(sent_rounds()):
        for s in range(NB):
            for b in range(BLK):
                at = (i * NB + s) * BLK + b
                hit = jnp.where(send_now[0, s, r] == b, 1.0, 0.0)
                place[at : at + 1, :] = jnp.full((1, BS), hit, F32)


def hid_part(k, size, self_w, neigh_w, low, back):
    at = rows(jnp.bitwise_xor(lax.axis_index("hid"), k), size)
    over_hidden = ((1,), (1,))
    return dot(self_w[at, :], low, over_hidden) + dot(neigh_w[at, :], back, over_hidden)


def back_kernel(
    place, start, low, self_w, neigh_w, got0, got1, got2, got3, own, far, give1, give3
):
    size, hidden = own.shape[0], start.shape[1]
    blocks = []
    for b in range(BLK):
        total = start[b * BS : (b + 1) * BS, :]
        for i, got in enumerate((got0, got1, got2, got3)):
            for s in range(NB):
                at = (i * NB + s) * BLK + b
                hit = jnp.concatenate([place[at : at + 1, :]] * (hidden // BS), axis=1)
                total = total + hit * got[s * BS : (s + 1) * BS, :].astype(F32)
        blocks.append(total.astype(BF16))
    back = jnp.concatenate(blocks, axis=0)
    part = functools.partial(hid_part, size=size, self_w=self_w, neigh_w=neigh_w)
    low_now = low[...]
    far[...] = part(2, low=low_now, back=back).astype(BF16)
    give1[...] = part(1, low=low_now, back=back).astype(BF16)
    give3[...] = part(3, low=low_now, back=back).astype(BF16)
    own[...] = part(0, low=low_now, back=back)


def on_device(
    features,
    self_weight,
    neigh_weight,
    cotangent,
    neighbor_blocks,
    local_tiles,
    send_blocks,
    recv_blocks,
    live_slots,
    boundary_tiles,
):
    n, width = features.shape
    hidden = self_weight.shape[1]
    slots = ROUNDS * NB * BS
    send_blocks = jnp.swapaxes(send_blocks, 1, 2)
    recv_blocks = jnp.swapaxes(recv_blocks, 1, 2)
    *packed, feats_now = call(
        pack_kernel,
        [((NB * BS // HID if r == 1 else NB * BS, width), BF16) for r in range(ROUNDS)]
        + [((n, width), BF16)],
        [HBM] * 2,
        nbytes=2_000_000,
        scratch=[pltpu.SMEM((1, NB, ROUNDS), jnp.int32), DMA((2,))],
    )(in_hbm(send_blocks), in_hbm(features))
    got_c, share, got_d, got_a = swaps(packed)
    (turned,) = call(
        turn_kernel, [((width, n), BF16)], [VMEM], flops=COVER_FLOPS, nbytes=2_000_000
    )(feats_now)
    share, got_a, turned = lax.optimization_barrier((share, got_a, turned))
    shares = [share] + [hid_swap(share, k) for k in (3, 1, 2)]
    local, edge, local_sum, inverse, own_pre = call(
        before_kernel,
        [
            ((n, n), BF16),
            ((n, slots), BF16),
            ((n, width), F32),
            ((n, BS), F32),
            ((n, hidden), F32),
        ],
        [HBM] * 6 + [VMEM] * 2,
        flops=COVER_FLOPS,
        nbytes=6_000_000,
        scratch=[
            pltpu.SMEM((1, BLK, K_IN), jnp.int32),
            pltpu.SMEM((1, NB, ROUNDS), jnp.int32),
            pltpu.SMEM((1, ROUNDS), jnp.int32),
            pltpu.VMEM((width, hidden), BF16),
            pltpu.VMEM((1, BLK, K_IN, BS, BS), BF16),
            pltpu.VMEM((1, ROUNDS, NB, BS, BS), BF16),
            DMA((6,)),
        ],
    )(
        in_hbm(neighbor_blocks),
        in_hbm(recv_blocks),
        in_hbm(live_slots),
        in_hbm(self_weight),
        in_hbm(local_tiles),
        in_hbm(boundary_tiles),
        feats_now,
        got_a,
    )
    act, low, spread, mean, give = call(
        middle_kernel,
        [((n, hidden), BF16)] * 3 + [((n, width), BF16), ((width, hidden), BF16)],
        [VMEM] * 13,
        flops=1_600_000_000,
        nbytes=8_000_000,
        scratch=[pltpu.VMEM((NB * BS, width), BF16)],
        limit=16,
    )(edge, got_c, got_d, *shares, local_sum, inverse, own_pre, neigh_weight, cotangent, turned)

    got = dom_swap(give, 1)
    (keep,) = call(
        keep_kernel, [((width, hidden), F32)], [VMEM] * 3, flops=200_000_000, nbytes=2_000_000
    )(turned, mean, low)
    got, keep = lax.optimization_barrier((got, keep))
    pieces = (CHIPS,) + PIECE
    (cut,) = call(cut_kernel, [(pieces, BF16)], [VMEM] * 2, nbytes=1_500_000)(keep, got)
    cut, spread, low = lax.optimization_barrier((cut, spread, low))
    *terms, activated, back, self_now, neigh_now, place = call(
        back_own_kernel,
        [((NB * BS, hidden), BF16)] * ROUNDS
        + [((n, hidden), BF16), ((n, hidden), F32)]
        + [((width, hidden), BF16)] * 2
        + [((ROUNDS * NB * BLK, BS), F32)],
        [HBM] + [VMEM] * 6,
        flops=600_000_000,
        nbytes=3_000_000,
        scratch=[pltpu.SMEM((1, NB, ROUNDS), jnp.int32), DMA((1,))],
    )(in_hbm(send_blocks), edge, spread, act, local, self_weight, neigh_weight)
    returned = swaps(terms)
    (summed,) = call(sum_kernel, [(pieces, BF16)], [VMEM], nbytes=700_000)(exchange(cut))
    summed, back = lax.optimization_barrier((summed, back))
    shape = (width // HID, n)
    in_own, in_far, in_first, in_third = call(
        back_kernel,
        [(shape, F32)] + [(shape, BF16)] * 3,
        [VMEM] * 9,
        flops=COVER_FLOPS,
        nbytes=3_000_000,
    )(place, back, low, self_now, neigh_now, *returned)
    in_parts = [hid_swap(in_far, 2), hid_swap(in_first, 1), hid_swap(in_third, 3)]
    mine = exchange(summed)
    other = dom_swap(mine, 1)
    scale = 1.0 / math.sqrt(n * lax.axis_size("dom"))
    grad_self, grad_neigh = call(
        functools.partial(last_kernel, scale),
        [((width, hidden), F32)] * 2,
        [VMEM] * 2,
        nbytes=2_000_000,
    )(mine, other)
    grad_input = in_own
    for part in in_parts:
        grad_input = grad_input + part.astype(F32)
    return activated, grad_self, grad_neigh, grad_input.astype(BF16).T


def solution(mesh):
    return jax.shard_map(
        on_device,
        mesh=mesh,
        in_specs=(
            P("dom", None),
            P(None, "hid"),
            P(None, "hid"),
            P("dom", "hid"),
            P("dom", None, None),
            P("dom", None, None, None, None),
            P("dom", None, None),
            P("dom", None, None),
            P("dom", None),
            P("dom", None, None, None, None),
        ),
        out_specs=(P("dom", "hid"), P(None, "hid"), P(None, "hid"), P("dom", "hid")),
        check_vma=False,
    )
```

```python
import functools
import math

import jax
import jax.numpy as jnp
from jax import lax
from jax.experimental import pallas as pl
from jax.experimental.pallas import tpu as pltpu
from jax.sharding import PartitionSpec as P

BS = 128
BLK = 4
K_IN = 8
ROUNDS = 4
NB = 2
CORES = 2
Z = 8
X = 4
HID = 4
CHIPS = X * Z
PIECE = (40, 128)
COVER_FLOPS = 60_000_000_000
BF16 = jnp.bfloat16
F32 = jnp.float32

VMEM = pl.BlockSpec(memory_space=pltpu.VMEM)
HBM = pl.BlockSpec(memory_space=pltpu.MemorySpace.HBM)
DMA = pltpu.SemaphoreType.DMA


def dot(a, b, dims=((1,), (0,))):
    return lax.dot_general(a, b, (dims, ((), ())), preferred_element_type=F32)


def call(kernel, outs, specs, flops=0, nbytes=0, limit=12, scratch=()):
    return pl.pallas_call(
        kernel,
        out_shape=[jax.ShapeDtypeStruct(shape, dtype) for shape, dtype in outs],
        in_specs=specs,
        out_specs=[VMEM] * len(outs),
        scratch_shapes=list(scratch),
        compiler_params=pltpu.CompilerParams(vmem_limit_bytes=limit * 1024 * 1024),
        cost_estimate=pl.CostEstimate(flops=flops, bytes_accessed=nbytes, transcendentals=0),
    )


def dom_swap(array, mask):
    count = lax.axis_size("dom")
    return lax.ppermute(array, "dom", [(i, i ^ mask) for i in range(count)])


def dom_pairs(array, step):
    count = lax.axis_size("dom")
    odd = [i for i in range(count) if (i // step) % 2]
    pairs = [(i, (i + step) % count) for i in odd]
    return lax.ppermute(array, "dom", pairs + [(j, i) for i, j in pairs])


def hid_swap(array, mask):
    return lax.ppermute(array, "hid", [(i, i ^ mask) for i in range(HID)])


def exchange(array):
    chips = [x * Z + z for x in (1, 2, 3, 0) for z in reversed(range(Z))]
    groups = [[CORES * chip + core for chip in chips] for core in range(CORES)]
    return lax.all_to_all(array, "dom", 0, 0, axis_index_groups=groups)


def in_hbm(array):
    return pltpu.with_memory_space_constraint(array, pltpu.MemorySpace.HBM)


def rows(block, size=BS):
    return pl.ds(pl.multiple_of(block * size, size), size)


def swaps(arrays):
    a, b, c, d = arrays
    return [dom_pairs(a, 2), dom_pairs(b, 1), dom_swap(c, 2), dom_swap(d, 1)]


def sent_rounds():
    me = lax.axis_index("dom")
    core, chip = lax.rem(me, CORES), lax.rem(me // CORES, 2)
    return (3 - chip, 1 - core, 2 + chip, core)


def received_rounds():
    first, second, third, fourth = sent_rounds()
    return (5 - first, 1 - second, 5 - third, 1 - fourth)


def pack_kernel(send, feats, out0, out1, out2, out3, feats_now, send_now, sems):
    copies = [
        pltpu.make_async_copy(send, send_now, sems.at[0]),
        pltpu.make_async_copy(feats, feats_now, sems.at[1]),
    ]
    for copy in copies:
        copy.start()
    for copy in copies:
        copy.wait()
    y, size = lax.axis_index("hid"), out1.shape[0]
    per_slot = HID // NB
    for r, out in zip(sent_rounds(), (out0, out1, out2, out3)):
        if out is out1:
            at = send_now[0, y // per_slot, r] * BS + lax.rem(y, per_slot) * size
            out[...] = feats_now[pl.ds(pl.multiple_of(at, size), size), :]
            continue
        for s in range(NB):
            out[s * BS : (s + 1) * BS, :] = feats_now[rows(send_now[0, s, r]), :]


def turn_kernel(feats, turned):
    turned[...] = feats[...].T


def before_kernel(
    neighbors,
    recv,
    live,
    self_w,
    tiles,
    edge_tiles,
    feats,
    got,
    local,
    edge,
    local_sum,
    inverse,
    own_pre,
    neighbors_now,
    recv_now,
    live_now,
    self_w_now,
    tiles_now,
    edge_tiles_now,
    sems,
):
    pairs = (
        (self_w, self_w_now),
        (neighbors, neighbors_now),
        (recv, recv_now),
        (live, live_now),
        (tiles, tiles_now),
        (edge_tiles, edge_tiles_now),
    )
    copies = [pltpu.make_async_copy(a, b, sems.at[i]) for i, (a, b) in enumerate(pairs)]
    for copy in copies:
        copy.start()
    local[...] = jnp.zeros_like(local)
    edge[...] = jnp.zeros_like(edge)
    copies[0].wait()
    mine = feats[...]
    own_pre[...] = dot(mine, self_w_now[...])
    for copy in copies[1:]:
        copy.wait()
    for b in range(BLK):
        for k in range(K_IN):
            cols = rows(neighbors_now[0, b, k])
            here = slice(b * BS, (b + 1) * BS)
            local[here, cols] = local[here, cols] + tiles_now[0, b, k]
    for i, r in enumerate(received_rounds()):
        for s in range(NB):
            slot = i * NB + s

            @pl.when(s < live_now[0, r])
            def _():
                edge[rows(recv_now[0, s, r]), slot * BS : (slot + 1) * BS] = edge_tiles_now[0, r, s]

    whole = local[...]
    of_pair = (ROUNDS - 1) * NB * BS
    local_sum[...] = dot(whole, mine) + dot(edge[:, of_pair:], got[...])
    ones = jnp.ones((BS * BLK, BS), BF16)
    edge_ones = jnp.ones((BS * NB * ROUNDS, BS), BF16)
    inverse[...] = 1.0 / (dot(whole, ones) + dot(edge[...], edge_ones))


def middle_kernel(
    edge,
    got0,
    got2,
    share0,
    share1,
    share2,
    share3,
    local_sum,
    inverse_in,
    own_pre,
    neigh_w,
    cot,
    turned,
    activated,
    low_out,
    spread_out,
    mean_out,
    give,
    got1,
):
    size = share0.shape[0]
    for k, share in zip((0, 3, 1, 2), (share0, share1, share2, share3)):
        got1[rows(jnp.bitwise_xor(lax.axis_index("hid"), k), size), :] = share[...]
    core = lax.rem(lax.axis_index("dom"), CORES)
    width = NB * BS
    total = local_sum[...]
    for r, got in enumerate((got0, got1, got2)):
        total = total + dot(edge[:, r * width : (r + 1) * width], got[...])
    inverse = inverse_in[...]
    mean = total * jnp.concatenate([inverse] * (total.shape[1] // BS), axis=1)
    mean_high = mean.astype(BF16)
    mean_rest = (mean - mean_high.astype(F32)).astype(BF16)
    weights = neigh_w[...]
    pre = own_pre[...] + dot(mean_high, weights) + dot(mean_rest, weights)
    sig = jax.nn.sigmoid(pre)
    activated[...] = (pre * sig).astype(BF16)
    grad = cot[...].astype(F32) * sig * (1.0 + pre * (1.0 - sig))
    low = grad.astype(BF16)
    low_out[...] = low
    spread = (grad * jnp.concatenate([inverse] * (grad.shape[1] // BS), axis=1)).astype(BF16)
    spread_out[...] = spread
    mean_out[...] = mean_high

    @pl.when(core == 0)
    def _():
        give[...] = dot(mean_high, low, ((0,), (0,))).astype(BF16)

    @pl.when(core == 1)
    def _():
        give[...] = dot(turned[...], low).astype(BF16)


def keep_kernel(turned, mean, low, keep):
    core = lax.rem(lax.axis_index("dom"), CORES)

    @pl.when(core == 0)
    def _():
        keep[...] = dot(turned[...], low[...])

    @pl.when(core == 1)
    def _():
        keep[...] = dot(mean[...], low[...], ((0,), (0,)))


def piece_at(i):
    return (i % 16) * PIECE[0], (i // 16) * PIECE[1]


def cut_kernel(keep, got, out):
    total = keep[...] + got[...].astype(F32)
    for i in range(CHIPS):
        at, lane = piece_at(i)
        out[i] = total[at : at + PIECE[0], lane : lane + PIECE[1]].astype(BF16)


def sum_kernel(got, out):
    done = jnp.sum(got[...].astype(F32), axis=0).astype(BF16)
    for i in range(CHIPS):
        out[i] = done


def last_kernel(scale, mine, other, of_self, of_neigh):
    core = lax.rem(lax.axis_index("dom"), CORES)

    def put(a, out):
        for i in range(CHIPS):
            at, lane = piece_at(i)
            out[at : at + PIECE[0], lane : lane + PIECE[1]] = a[i].astype(F32) * scale

    @pl.when(core == 0)
    def _():
        put(mine, of_self)
        put(other, of_neigh)

    @pl.when(core == 1)
    def _():
        put(other, of_self)
        put(mine, of_neigh)


def back_own_kernel(
    send,
    edge,
    spread,
    act,
    local,
    self_w,
    neigh_w,
    term0,
    term1,
    term2,
    term3,
    activated,
    back,
    self_w_out,
    neigh_w_out,
    place,
    send_now,
    sem,
):
    copy = pltpu.make_async_copy(send, send_now, sem.at[0])
    copy.start()
    over_rows = ((0,), (0,))
    width = NB * BS
    for r, term in enumerate((term0, term1, term2, term3)):
        of_round = edge[:, r * width : (r + 1) * width]
        term[...] = dot(of_round, spread[...], over_rows).astype(BF16)
    activated[...] = act[...]
    back[...] = dot(local[...], spread[...], over_rows)
    self_w_out[...] = self_w[...]
    neigh_w_out[...] = neigh_w[...]
    copy.wait()
    for i, r in enumerate(sent_rounds()):
        for s in range(NB):
            for b in range(BLK):
                at = (i * NB + s) * BLK + b
                hit = jnp.where(send_now[0, s, r] == b, 1.0, 0.0)
                place[at : at + 1, :] = jnp.full((1, BS), hit, F32)


def hid_part(k, size, self_w, neigh_w, low, back):
    at = rows(jnp.bitwise_xor(lax.axis_index("hid"), k), size)
    over_hidden = ((1,), (1,))
    return dot(self_w[at, :], low, over_hidden) + dot(neigh_w[at, :], back, over_hidden)


def back_kernel(
    place, start, low, self_w, neigh_w, got0, got1, got2, got3, own, far, give1, give3
):
    size, hidden = own.shape[0], start.shape[1]
    blocks = []
    for b in range(BLK):
        total = start[b * BS : (b + 1) * BS, :]
        for i, got in enumerate((got0, got1, got2, got3)):
            for s in range(NB):
                at = (i * NB + s) * BLK + b
                hit = jnp.concatenate([place[at : at + 1, :]] * (hidden // BS), axis=1)
                total = total + hit * got[s * BS : (s + 1) * BS, :].astype(F32)
        blocks.append(total.astype(BF16))
    back = jnp.concatenate(blocks, axis=0)
    part = functools.partial(hid_part, size=size, self_w=self_w, neigh_w=neigh_w)
    low_now = low[...]
    far[...] = part(2, low=low_now, back=back).astype(BF16)
    give1[...] = part(1, low=low_now, back=back).astype(BF16)
    give3[...] = part(3, low=low_now, back=back).astype(BF16)
    own[...] = part(0, low=low_now, back=back)


def on_device(
    features,
    self_weight,
    neigh_weight,
    cotangent,
    neighbor_blocks,
    local_tiles,
    send_blocks,
    recv_blocks,
    live_slots,
    boundary_tiles,
):
    n, width = features.shape
    hidden = self_weight.shape[1]
    slots = ROUNDS * NB * BS
    send_blocks = jnp.swapaxes(send_blocks, 1, 2)
    recv_blocks = jnp.swapaxes(recv_blocks, 1, 2)
    *packed, feats_now = call(
        pack_kernel,
        [((NB * BS // HID if r == 1 else NB * BS, width), BF16) for r in range(ROUNDS)]
        + [((n, width), BF16)],
        [HBM] * 2,
        nbytes=2_000_000,
        scratch=[pltpu.SMEM((1, NB, ROUNDS), jnp.int32), DMA((2,))],
    )(in_hbm(send_blocks), in_hbm(features))
    got_c, share, got_d, got_a = swaps(packed)
    (turned,) = call(
        turn_kernel, [((width, n), BF16)], [VMEM], flops=COVER_FLOPS, nbytes=2_000_000
    )(feats_now)
    share, got_a, turned = lax.optimization_barrier((share, got_a, turned))
    shares = [share] + [hid_swap(share, k) for k in (3, 1, 2)]
    local, edge, local_sum, inverse, own_pre = call(
        before_kernel,
        [
            ((n, n), BF16),
            ((n, slots), BF16),
            ((n, width), F32),
            ((n, BS), F32),
            ((n, hidden), F32),
        ],
        [HBM] * 6 + [VMEM] * 2,
        flops=COVER_FLOPS,
        nbytes=6_000_000,
        scratch=[
            pltpu.SMEM((1, BLK, K_IN), jnp.int32),
            pltpu.SMEM((1, NB, ROUNDS), jnp.int32),
            pltpu.SMEM((1, ROUNDS), jnp.int32),
            pltpu.VMEM((width, hidden), BF16),
            pltpu.VMEM((1, BLK, K_IN, BS, BS), BF16),
            pltpu.VMEM((1, ROUNDS, NB, BS, BS), BF16),
            DMA((6,)),
        ],
    )(
        in_hbm(neighbor_blocks),
        in_hbm(recv_blocks),
        in_hbm(live_slots),
        in_hbm(self_weight),
        in_hbm(local_tiles),
        in_hbm(boundary_tiles),
        feats_now,
        got_a,
    )
    act, low, spread, mean, give = call(
        middle_kernel,
        [((n, hidden), BF16)] * 3 + [((n, width), BF16), ((width, hidden), BF16)],
        [VMEM] * 13,
        flops=1_600_000_000,
        nbytes=8_000_000,
        scratch=[pltpu.VMEM((NB * BS, width), BF16)],
        limit=16,
    )(edge, got_c, got_d, *shares, local_sum, inverse, own_pre, neigh_weight, cotangent, turned)

    got = dom_swap(give, 1)
    (keep,) = call(
        keep_kernel, [((width, hidden), F32)], [VMEM] * 3, flops=200_000_000, nbytes=2_000_000
    )(turned, mean, low)
    got, keep = lax.optimization_barrier((got, keep))
    pieces = (CHIPS,) + PIECE
    (cut,) = call(cut_kernel, [(pieces, BF16)], [VMEM] * 2, nbytes=1_500_000)(keep, got)
    cut, spread, low = lax.optimization_barrier((cut, spread, low))
    *terms, activated, back, self_now, neigh_now, place = call(
        back_own_kernel,
        [((NB * BS, hidden), BF16)] * ROUNDS
        + [((n, hidden), BF16), ((n, hidden), F32)]
        + [((width, hidden), BF16)] * 2
        + [((ROUNDS * NB * BLK, BS), F32)],
        [HBM] + [VMEM] * 6,
        flops=600_000_000,
        nbytes=3_000_000,
        scratch=[pltpu.SMEM((1, NB, ROUNDS), jnp.int32), DMA((1,))],
    )(in_hbm(send_blocks), edge, spread, act, local, self_weight, neigh_weight)
    returned = swaps(terms)
    (summed,) = call(sum_kernel, [(pieces, BF16)], [VMEM], nbytes=700_000)(exchange(cut))
    summed, back = lax.optimization_barrier((summed, back))
    shape = (width // HID, n)
    in_own, in_far, in_first, in_third = call(
        back_kernel,
        [(shape, F32)] + [(shape, BF16)] * 3,
        [VMEM] * 9,
        flops=COVER_FLOPS,
        nbytes=3_000_000,
    )(place, back, low, self_now, neigh_now, *returned)
    in_parts = [hid_swap(in_far, 2), hid_swap(in_first, 1), hid_swap(in_third, 3)]
    mine = exchange(summed)
    other = dom_swap(mine, 1)
    scale = 1.0 / math.sqrt(n * lax.axis_size("dom"))
    grad_self, grad_neigh = call(
        functools.partial(last_kernel, scale),
        [((width, hidden), F32)] * 2,
        [VMEM] * 2,
        nbytes=2_000_000,
    )(mine, other)
    grad_input = in_own
    for part in in_parts:
        grad_input = grad_input + part.astype(F32)
    return activated, grad_self, grad_neigh, grad_input.astype(BF16).T


def solution(mesh):
    return jax.shard_map(
        on_device,
        mesh=mesh,
        in_specs=(
            P("dom", None),
            P(None, "hid"),
            P(None, "hid"),
            P("dom", "hid"),
            P("dom", None, None),
            P("dom", None, None, None, None),
            P("dom", None, None),
            P("dom", None, None),
            P("dom", None),
            P("dom", None, None, None, None),
        ),
        out_specs=(P("dom", "hid"), P(None, "hid"), P(None, "hid"), P("dom", "hid")),
        check_vma=False,
    )
```

```python
import functools
import math

import jax
import jax.numpy as jnp
from jax import lax
from jax.experimental import pallas as pl
from jax.experimental.pallas import tpu as pltpu
from jax.sharding import PartitionSpec as P

BS = 128
BLK = 4
K_IN = 8
ROUNDS = 4
NB = 2
CORES = 2
Z = 8
X = 4
HID = 4
CHIPS = X * Z
PIECE = (40, 128)
GROUPS = 4
COVER_FLOPS = 60_000_000_000
BF16 = jnp.bfloat16
F32 = jnp.float32

VMEM = pl.BlockSpec(memory_space=pltpu.VMEM)
HBM = pl.BlockSpec(memory_space=pltpu.MemorySpace.HBM)
DMA = pltpu.SemaphoreType.DMA


def dot(a, b, dims=((1,), (0,))):
    return lax.dot_general(a, b, (dims, ((), ())), preferred_element_type=F32)


def call(kernel, outs, specs, flops=0, nbytes=0, limit=12, scratch=(), out_specs=None):
    return pl.pallas_call(
        kernel,
        out_shape=[jax.ShapeDtypeStruct(shape, dtype) for shape, dtype in outs],
        in_specs=specs,
        out_specs=out_specs or [VMEM] * len(outs),
        scratch_shapes=list(scratch),
        compiler_params=pltpu.CompilerParams(vmem_limit_bytes=limit * 1024 * 1024),
        cost_estimate=pl.CostEstimate(flops=flops, bytes_accessed=nbytes, transcendentals=0),
    )


def dom_swap(array, mask):
    count = lax.axis_size("dom")
    return lax.ppermute(array, "dom", [(i, i ^ mask) for i in range(count)])


def dom_pairs(array, step):
    count = lax.axis_size("dom")
    odd = [i for i in range(count) if (i // step) % 2]
    pairs = [(i, (i + step) % count) for i in odd]
    return lax.ppermute(array, "dom", pairs + [(j, i) for i, j in pairs])


def hid_swap(array, mask):
    return lax.ppermute(array, "hid", [(i, i ^ mask) for i in range(HID)])


def exchange(array):
    chips = [x * Z + z for x in (1, 2, 3, 0) for z in reversed(range(Z))]
    groups = [[CORES * chip + core for chip in chips] for core in range(CORES)]
    return lax.all_to_all(array, "dom", 0, 0, axis_index_groups=groups)


def in_hbm(array):
    return pltpu.with_memory_space_constraint(array, pltpu.MemorySpace.HBM)


def rows(block, size=BS):
    return pl.ds(pl.multiple_of(block * size, size), size)


def swaps(arrays):
    a, b, c, d = arrays
    return [dom_pairs(a, 2), dom_pairs(b, 1), dom_swap(c, 2), dom_swap(d, 1)]


def sent_rounds():
    me = lax.axis_index("dom")
    core, chip = lax.rem(me, CORES), lax.rem(me // CORES, 2)
    return (3 - chip, 1 - core, 2 + chip, core)


def received_rounds():
    first, second, third, fourth = sent_rounds()
    return (5 - first, 1 - second, 5 - third, 1 - fourth)


def pack_kernel(send, feats, out0, out1, out2, out3, feats_now, send_now, sems):
    copies = [
        pltpu.make_async_copy(send, send_now, sems.at[0]),
        pltpu.make_async_copy(feats, feats_now, sems.at[1]),
    ]
    for copy in copies:
        copy.start()
    for copy in copies:
        copy.wait()
    y, size = lax.axis_index("hid"), out1.shape[0]
    per_slot = HID // NB
    for r, out in zip(sent_rounds(), (out0, out1, out2, out3)):
        if out is out1:
            at = send_now[0, y // per_slot, r] * BS + lax.rem(y, per_slot) * size
            out[...] = feats_now[pl.ds(pl.multiple_of(at, size), size), :]
            continue
        for s in range(NB):
            out[s * BS : (s + 1) * BS, :] = feats_now[rows(send_now[0, s, r]), :]


def turn_kernel(feats, turned):
    turned[...] = feats[...].T


def before_kernel(
    neighbors,
    recv,
    live,
    self_w,
    tiles,
    edge_tiles,
    feats,
    got,
    local,
    edge,
    local_sum,
    inverse,
    own_pre,
    neighbors_now,
    recv_now,
    live_now,
    self_w_now,
    tiles_now,
    edge_tiles_now,
    sems,
):
    pairs = (
        (self_w, self_w_now),
        (neighbors, neighbors_now),
        (recv, recv_now),
        (live, live_now),
        (tiles, tiles_now),
        (edge_tiles, edge_tiles_now),
    )
    copies = [pltpu.make_async_copy(a, b, sems.at[i]) for i, (a, b) in enumerate(pairs)]
    for copy in copies:
        copy.start()
    local[...] = jnp.zeros_like(local)
    edge[...] = jnp.zeros_like(edge)
    copies[0].wait()
    mine = feats[...]
    own_pre[...] = dot(mine, self_w_now[...])
    for copy in copies[1:]:
        copy.wait()
    for b in range(BLK):
        for k in range(K_IN):
            cols = rows(neighbors_now[0, b, k])
            here = slice(b * BS, (b + 1) * BS)
            local[here, cols] = local[here, cols] + tiles_now[0, b, k]
    for i, r in enumerate(received_rounds()):
        for s in range(NB):
            slot = i * NB + s

            @pl.when(s < live_now[0, r])
            def _():
                edge[rows(recv_now[0, s, r]), slot * BS : (slot + 1) * BS] = edge_tiles_now[0, r, s]

    whole = local[...]
    of_pair = (ROUNDS - 1) * NB * BS
    local_sum[...] = dot(whole, mine) + dot(edge[:, of_pair:], got[...])
    ones = jnp.ones((BS * BLK, BS), BF16)
    edge_ones = jnp.ones((BS * NB * ROUNDS, BS), BF16)
    inverse[...] = 1.0 / (dot(whole, ones) + dot(edge[...], edge_ones))


def middle_kernel(
    edge,
    got0,
    got2,
    share0,
    share1,
    share2,
    share3,
    local_sum,
    inverse_in,
    own_pre,
    neigh_w,
    cot,
    turned,
    activated,
    low_out,
    spread_out,
    mean_out,
    give,
    got1,
):
    size = share0.shape[0]
    for k, share in zip((0, 3, 1, 2), (share0, share1, share2, share3)):
        got1[rows(jnp.bitwise_xor(lax.axis_index("hid"), k), size), :] = share[...]
    core = lax.rem(lax.axis_index("dom"), CORES)
    width = NB * BS
    total = local_sum[...]
    for r, got in enumerate((got0, got1, got2)):
        total = total + dot(edge[:, r * width : (r + 1) * width], got[...])
    inverse = inverse_in[...]
    mean = total * jnp.concatenate([inverse] * (total.shape[1] // BS), axis=1)
    mean_high = mean.astype(BF16)
    mean_rest = (mean - mean_high.astype(F32)).astype(BF16)
    weights = neigh_w[...]
    pre = own_pre[...] + dot(mean_high, weights) + dot(mean_rest, weights)
    sig = jax.nn.sigmoid(pre)
    activated[...] = (pre * sig).astype(BF16)
    grad = cot[...].astype(F32) * sig * (1.0 + pre * (1.0 - sig))
    low = grad.astype(BF16)
    low_out[...] = low
    spread = (grad * jnp.concatenate([inverse] * (grad.shape[1] // BS), axis=1)).astype(BF16)
    spread_out[...] = spread
    mean_out[...] = mean_high

    @pl.when(core == 0)
    def _():
        give[...] = dot(mean_high, low, ((0,), (0,))).astype(BF16)

    @pl.when(core == 1)
    def _():
        give[...] = dot(turned[...], low).astype(BF16)


def keep_kernel(turned, mean, low, keep):
    core = lax.rem(lax.axis_index("dom"), CORES)

    @pl.when(core == 0)
    def _():
        keep[...] = dot(turned[...], low[...])

    @pl.when(core == 1)
    def _():
        keep[...] = dot(mean[...], low[...], ((0,), (0,)))


def piece_at(i):
    return (i % 16) * PIECE[0], (i // 16) * PIECE[1]


def cut_kernel(keep, got, out, buffer, sems):
    total = keep[...] + got[...].astype(F32)
    copies = []
    span = CHIPS // GROUPS
    for group in range(GROUPS):
        for i in range(group * span, (group + 1) * span):
            at, lane = piece_at(i)
            buffer[i] = total[at : at + PIECE[0], lane : lane + PIECE[1]].astype(BF16)
        here = pl.ds(group * span, span)
        copies.append(pltpu.make_async_copy(buffer.at[here], out.at[here], sems.at[group]))
        copies[-1].start()
    for copy in copies:
        copy.wait()


def sum_kernel(got, out, got_now, buffer, sems):
    span = CHIPS // GROUPS
    parts = [pl.ds(group * span, span) for group in range(GROUPS)]
    copies = [
        pltpu.make_async_copy(got.at[part], got_now.at[part], sems.at[group])
        for group, part in enumerate(parts)
    ]
    for copy in copies:
        copy.start()
    total = jnp.zeros(PIECE, F32)
    for part, copy in zip(parts, copies):
        copy.wait()
        total = total + jnp.sum(got_now[part].astype(F32), axis=0)
    done = total.astype(BF16)
    for i in range(span):
        buffer[i] = done
    copies = [
        pltpu.make_async_copy(buffer, out.at[part], sems.at[GROUPS + group])
        for group, part in enumerate(parts)
    ]
    for copy in copies:
        copy.start()
    for copy in copies:
        copy.wait()


def last_kernel(scale, mine, other, of_self, of_neigh):
    core = lax.rem(lax.axis_index("dom"), CORES)

    def put(a, out):
        for i in range(CHIPS):
            at, lane = piece_at(i)
            out[at : at + PIECE[0], lane : lane + PIECE[1]] = a[i].astype(F32) * scale

    @pl.when(core == 0)
    def _():
        put(mine, of_self)
        put(other, of_neigh)

    @pl.when(core == 1)
    def _():
        put(other, of_self)
        put(mine, of_neigh)


def back_own_kernel(
    send,
    edge,
    spread,
    act,
    local,
    self_w,
    neigh_w,
    term0,
    term1,
    term2,
    term3,
    activated,
    back,
    self_w_out,
    neigh_w_out,
    place,
    send_now,
    sem,
):
    copy = pltpu.make_async_copy(send, send_now, sem.at[0])
    copy.start()
    over_rows = ((0,), (0,))
    width = NB * BS
    for r, term in enumerate((term0, term1, term2, term3)):
        of_round = edge[:, r * width : (r + 1) * width]
        term[...] = dot(of_round, spread[...], over_rows).astype(BF16)
    activated[...] = act[...]
    back[...] = dot(local[...], spread[...], over_rows)
    self_w_out[...] = self_w[...]
    neigh_w_out[...] = neigh_w[...]
    copy.wait()
    for i, r in enumerate(sent_rounds()):
        for s in range(NB):
            for b in range(BLK):
                at = (i * NB + s) * BLK + b
                hit = jnp.where(send_now[0, s, r] == b, 1.0, 0.0)
                place[at : at + 1, :] = jnp.full((1, BS), hit, F32)


def hid_part(k, size, self_w, neigh_w, low, back):
    at = rows(jnp.bitwise_xor(lax.axis_index("hid"), k), size)
    over_hidden = ((1,), (1,))
    return dot(self_w[at, :], low, over_hidden) + dot(neigh_w[at, :], back, over_hidden)


def back_kernel(
    place, start, low, self_w, neigh_w, got0, got1, got2, got3, own, far, give1, give3
):
    size, hidden = own.shape[0], start.shape[1]
    blocks = []
    for b in range(BLK):
        total = start[b * BS : (b + 1) * BS, :]
        for i, got in enumerate((got0, got1, got2, got3)):
            for s in range(NB):
                at = (i * NB + s) * BLK + b
                hit = jnp.concatenate([place[at : at + 1, :]] * (hidden // BS), axis=1)
                total = total + hit * got[s * BS : (s + 1) * BS, :].astype(F32)
        blocks.append(total.astype(BF16))
    back = jnp.concatenate(blocks, axis=0)
    part = functools.partial(hid_part, size=size, self_w=self_w, neigh_w=neigh_w)
    low_now = low[...]
    far[...] = part(2, low=low_now, back=back).astype(BF16)
    give1[...] = part(1, low=low_now, back=back).astype(BF16)
    give3[...] = part(3, low=low_now, back=back).astype(BF16)
    own[...] = part(0, low=low_now, back=back)


def on_device(
    features,
    self_weight,
    neigh_weight,
    cotangent,
    neighbor_blocks,
    local_tiles,
    send_blocks,
    recv_blocks,
    live_slots,
    boundary_tiles,
):
    n, width = features.shape
    hidden = self_weight.shape[1]
    slots = ROUNDS * NB * BS
    send_blocks = jnp.swapaxes(send_blocks, 1, 2)
    recv_blocks = jnp.swapaxes(recv_blocks, 1, 2)
    *packed, feats_now = call(
        pack_kernel,
        [((NB * BS // HID if r == 1 else NB * BS, width), BF16) for r in range(ROUNDS)]
        + [((n, width), BF16)],
        [HBM] * 2,
        nbytes=2_000_000,
        scratch=[pltpu.SMEM((1, NB, ROUNDS), jnp.int32), DMA((2,))],
    )(in_hbm(send_blocks), in_hbm(features))
    got_c, share, got_d, got_a = swaps(packed)
    (turned,) = call(
        turn_kernel, [((width, n), BF16)], [VMEM], flops=COVER_FLOPS, nbytes=2_000_000
    )(feats_now)
    share, got_a, turned = lax.optimization_barrier((share, got_a, turned))
    shares = [share] + [hid_swap(share, k) for k in (3, 1, 2)]
    local, edge, local_sum, inverse, own_pre = call(
        before_kernel,
        [
            ((n, n), BF16),
            ((n, slots), BF16),
            ((n, width), F32),
            ((n, BS), F32),
            ((n, hidden), F32),
        ],
        [HBM] * 6 + [VMEM] * 2,
        flops=COVER_FLOPS,
        nbytes=6_000_000,
        scratch=[
            pltpu.SMEM((1, BLK, K_IN), jnp.int32),
            pltpu.SMEM((1, NB, ROUNDS), jnp.int32),
            pltpu.SMEM((1, ROUNDS), jnp.int32),
            pltpu.VMEM((width, hidden), BF16),
            pltpu.VMEM((1, BLK, K_IN, BS, BS), BF16),
            pltpu.VMEM((1, ROUNDS, NB, BS, BS), BF16),
            DMA((6,)),
        ],
    )(
        in_hbm(neighbor_blocks),
        in_hbm(recv_blocks),
        in_hbm(live_slots),
        in_hbm(self_weight),
        in_hbm(local_tiles),
        in_hbm(boundary_tiles),
        feats_now,
        got_a,
    )
    act, low, spread, mean, give = call(
        middle_kernel,
        [((n, hidden), BF16)] * 3 + [((n, width), BF16), ((width, hidden), BF16)],
        [VMEM] * 13,
        flops=1_600_000_000,
        nbytes=8_000_000,
        scratch=[pltpu.VMEM((NB * BS, width), BF16)],
        limit=16,
    )(edge, got_c, got_d, *shares, local_sum, inverse, own_pre, neigh_weight, cotangent, turned)

    got = dom_swap(give, 1)
    (keep,) = call(
        keep_kernel, [((width, hidden), F32)], [VMEM] * 3, flops=200_000_000, nbytes=2_000_000
    )(turned, mean, low)
    got, keep = lax.optimization_barrier((got, keep))
    pieces = (CHIPS,) + PIECE
    (cut,) = call(
        cut_kernel,
        [(pieces, BF16)],
        [VMEM] * 2,
        nbytes=1_500_000,
        scratch=[pltpu.VMEM(pieces, BF16), DMA((GROUPS,))],
        out_specs=[HBM],
    )(keep, got)
    cut, spread, low = lax.optimization_barrier((cut, spread, low))
    *terms, activated, back, self_now, neigh_now, place = call(
        back_own_kernel,
        [((NB * BS, hidden), BF16)] * ROUNDS
        + [((n, hidden), BF16), ((n, hidden), F32)]
        + [((width, hidden), BF16)] * 2
        + [((ROUNDS * NB * BLK, BS), F32)],
        [HBM] + [VMEM] * 6,
        flops=600_000_000,
        nbytes=3_000_000,
        scratch=[pltpu.SMEM((1, NB, ROUNDS), jnp.int32), DMA((1,))],
    )(in_hbm(send_blocks), edge, spread, act, local, self_weight, neigh_weight)
    returned = swaps(terms)
    (summed,) = call(
        sum_kernel,
        [(pieces, BF16)],
        [HBM],
        nbytes=700_000,
        scratch=[
            pltpu.VMEM(pieces, BF16),
            pltpu.VMEM((CHIPS // GROUPS,) + PIECE, BF16),
            DMA((2 * GROUPS,)),
        ],
        out_specs=[HBM],
    )(in_hbm(exchange(cut)))
    summed, back = lax.optimization_barrier((summed, back))
    shape = (width // HID, n)
    in_own, in_far, in_first, in_third = call(
        back_kernel,
        [(shape, F32)] + [(shape, BF16)] * 3,
        [VMEM] * 9,
        flops=COVER_FLOPS,
        nbytes=3_000_000,
    )(place, back, low, self_now, neigh_now, *returned)
    in_parts = [hid_swap(in_far, 2), hid_swap(in_first, 1), hid_swap(in_third, 3)]
    mine = exchange(summed)
    other = dom_swap(mine, 1)
    scale = 1.0 / math.sqrt(n * lax.axis_size("dom"))
    grad_self, grad_neigh = call(
        functools.partial(last_kernel, scale),
        [((width, hidden), F32)] * 2,
        [VMEM] * 2,
        nbytes=2_000_000,
    )(mine, other)
    grad_input = in_own
    for part in in_parts:
        grad_input = grad_input + part.astype(F32)
    return activated, grad_self, grad_neigh, grad_input.astype(BF16).T


def solution(mesh):
    return jax.shard_map(
        on_device,
        mesh=mesh,
        in_specs=(
            P("dom", None),
            P(None, "hid"),
            P(None, "hid"),
            P("dom", "hid"),
            P("dom", None, None),
            P("dom", None, None, None, None),
            P("dom", None, None),
            P("dom", None, None),
            P("dom", None),
            P("dom", None, None, None, None),
        ),
        out_specs=(P("dom", "hid"), P(None, "hid"), P(None, "hid"), P("dom", "hid")),
        check_vma=False,
    )
```

```python
import functools
import math

import jax
import jax.numpy as jnp
from jax import lax
from jax.experimental import pallas as pl
from jax.experimental.pallas import tpu as pltpu
from jax.sharding import PartitionSpec as P

BS = 128
BLK = 4
K_IN = 8
ROUNDS = 4
NB = 2
CORES = 2
Z = 8
X = 4
HID = 4
CHIPS = X * Z
PIECE = (40, 128)
COVER_FLOPS = 60_000_000_000
BF16 = jnp.bfloat16
F32 = jnp.float32

VMEM = pl.BlockSpec(memory_space=pltpu.VMEM)
HBM = pl.BlockSpec(memory_space=pltpu.MemorySpace.HBM)
DMA = pltpu.SemaphoreType.DMA


def dot(a, b, dims=((1,), (0,))):
    return lax.dot_general(a, b, (dims, ((), ())), preferred_element_type=F32)


def call(kernel, outs, specs, flops=0, nbytes=0, limit=12, scratch=()):
    return pl.pallas_call(
        kernel,
        out_shape=[jax.ShapeDtypeStruct(shape, dtype) for shape, dtype in outs],
        in_specs=specs,
        out_specs=[VMEM] * len(outs),
        scratch_shapes=list(scratch),
        compiler_params=pltpu.CompilerParams(vmem_limit_bytes=limit * 1024 * 1024),
        cost_estimate=pl.CostEstimate(flops=flops, bytes_accessed=nbytes, transcendentals=0),
    )


def dom_swap(array, mask):
    count = lax.axis_size("dom")
    return lax.ppermute(array, "dom", [(i, i ^ mask) for i in range(count)])


def dom_pairs(array, step):
    count = lax.axis_size("dom")
    odd = [i for i in range(count) if (i // step) % 2]
    pairs = [(i, (i + step) % count) for i in odd]
    return lax.ppermute(array, "dom", pairs + [(j, i) for i, j in pairs])


def hid_swap(array, mask):
    return lax.ppermute(array, "hid", [(i, i ^ mask) for i in range(HID)])


def exchange(array):
    chips = [x * Z + z for x in (1, 2, 3, 0) for z in reversed(range(Z))]
    groups = [[CORES * chip + core for chip in chips] for core in range(CORES)]
    return lax.all_to_all(array, "dom", 0, 0, axis_index_groups=groups)


def in_hbm(array):
    return pltpu.with_memory_space_constraint(array, pltpu.MemorySpace.HBM)


def rows(block, size=BS):
    return pl.ds(pl.multiple_of(block * size, size), size)


def swaps(arrays):
    a, b, c, d = arrays
    return [dom_pairs(a, 2), dom_pairs(b, 1), dom_swap(c, 2), dom_swap(d, 1)]


def sent_rounds():
    me = lax.axis_index("dom")
    core, chip = lax.rem(me, CORES), lax.rem(me // CORES, 2)
    return (3 - chip, 1 - core, 2 + chip, core)


def received_rounds():
    first, second, third, fourth = sent_rounds()
    return (5 - first, 1 - second, 5 - third, 1 - fourth)


def pack_kernel(send, feats, out0, out1, out2, out3, feats_now, send_now, sems):
    copies = [
        pltpu.make_async_copy(send, send_now, sems.at[0]),
        pltpu.make_async_copy(feats, feats_now, sems.at[1]),
    ]
    for copy in copies:
        copy.start()
    for copy in copies:
        copy.wait()
    y, size = lax.axis_index("hid"), out1.shape[0]
    per_slot = HID // NB
    for r, out in zip(sent_rounds(), (out0, out1, out2, out3)):
        if out is out1:
            at = send_now[0, y // per_slot, r] * BS + lax.rem(y, per_slot) * size
            out[...] = feats_now[pl.ds(pl.multiple_of(at, size), size), :]
            continue
        for s in range(NB):
            out[s * BS : (s + 1) * BS, :] = feats_now[rows(send_now[0, s, r]), :]


def turn_kernel(feats, turned):
    turned[...] = feats[...].T


def before_kernel(
    neighbors,
    recv,
    live,
    self_w,
    tiles,
    edge_tiles,
    feats,
    got,
    local,
    edge,
    local_sum,
    inverse,
    own_pre,
    neighbors_now,
    recv_now,
    live_now,
    self_w_now,
    tiles_now,
    edge_tiles_now,
    sems,
):
    pairs = (
        (self_w, self_w_now),
        (neighbors, neighbors_now),
        (recv, recv_now),
        (live, live_now),
        (tiles, tiles_now),
        (edge_tiles, edge_tiles_now),
    )
    copies = [pltpu.make_async_copy(a, b, sems.at[i]) for i, (a, b) in enumerate(pairs)]
    for copy in copies:
        copy.start()
    local[...] = jnp.zeros_like(local)
    edge[...] = jnp.zeros_like(edge)
    copies[0].wait()
    mine = feats[...]
    own_pre[...] = dot(mine, self_w_now[...])
    for copy in copies[1:]:
        copy.wait()
    for b in range(BLK):
        for k in range(K_IN):
            cols = rows(neighbors_now[0, b, k])
            here = slice(b * BS, (b + 1) * BS)
            local[here, cols] = local[here, cols] + tiles_now[0, b, k]
    for i, r in enumerate(received_rounds()):
        for s in range(NB):
            slot = i * NB + s

            @pl.when(s < live_now[0, r])
            def _():
                edge[rows(recv_now[0, s, r]), slot * BS : (slot + 1) * BS] = edge_tiles_now[0, r, s]

    whole = local[...]
    of_pair = (ROUNDS - 1) * NB * BS
    local_sum[...] = dot(whole, mine) + dot(edge[:, of_pair:], got[...])
    ones = jnp.ones((BS * BLK, BS), BF16)
    edge_ones = jnp.ones((BS * NB * ROUNDS, BS), BF16)
    inverse[...] = 1.0 / (dot(whole, ones) + dot(edge[...], edge_ones))


def middle_kernel(
    edge,
    got0,
    got2,
    share0,
    share1,
    share2,
    share3,
    local_sum,
    inverse_in,
    own_pre,
    neigh_w,
    cot,
    turned,
    activated,
    low_out,
    spread_out,
    mean_out,
    give,
    got1,
):
    size = share0.shape[0]
    for k, share in zip((0, 3, 1, 2), (share0, share1, share2, share3)):
        got1[rows(jnp.bitwise_xor(lax.axis_index("hid"), k), size), :] = share[...]
    core = lax.rem(lax.axis_index("dom"), CORES)
    width = NB * BS
    total = local_sum[...]
    for r, got in enumerate((got0, got1, got2)):
        total = total + dot(edge[:, r * width : (r + 1) * width], got[...])
    inverse = inverse_in[...]
    mean = total * jnp.concatenate([inverse] * (total.shape[1] // BS), axis=1)
    mean_high = mean.astype(BF16)
    mean_rest = (mean - mean_high.astype(F32)).astype(BF16)
    weights = neigh_w[...]
    both = dot(jnp.concatenate([mean_high, mean_rest], axis=0), weights)
    count = mean.shape[0]
    pre = own_pre[...] + both[:count] + both[count:]
    sig = jax.nn.sigmoid(pre)
    activated[...] = (pre * sig).astype(BF16)
    grad = cot[...].astype(F32) * sig * (1.0 + pre * (1.0 - sig))
    low = grad.astype(BF16)
    low_out[...] = low
    spread = (grad * jnp.concatenate([inverse] * (grad.shape[1] // BS), axis=1)).astype(BF16)
    spread_out[...] = spread
    mean_out[...] = mean_high

    @pl.when(core == 0)
    def _():
        give[...] = dot(mean_high, low, ((0,), (0,))).astype(BF16)

    @pl.when(core == 1)
    def _():
        give[...] = dot(turned[...], low).astype(BF16)


def keep_kernel(turned, mean, low, keep):
    core = lax.rem(lax.axis_index("dom"), CORES)

    @pl.when(core == 0)
    def _():
        keep[...] = dot(turned[...], low[...])

    @pl.when(core == 1)
    def _():
        keep[...] = dot(mean[...], low[...], ((0,), (0,)))


def piece_at(i):
    return (i % 16) * PIECE[0], (i // 16) * PIECE[1]


def cut_kernel(keep, got, out):
    total = keep[...] + got[...].astype(F32)
    for i in range(CHIPS):
        at, lane = piece_at(i)
        out[i] = total[at : at + PIECE[0], lane : lane + PIECE[1]].astype(BF16)


def sum_kernel(got, out):
    done = jnp.sum(got[...].astype(F32), axis=0).astype(BF16)
    for i in range(CHIPS):
        out[i] = done


def last_kernel(scale, mine, other, of_self, of_neigh):
    core = lax.rem(lax.axis_index("dom"), CORES)

    def put(a, out):
        for i in range(CHIPS):
            at, lane = piece_at(i)
            out[at : at + PIECE[0], lane : lane + PIECE[1]] = a[i].astype(F32) * scale

    @pl.when(core == 0)
    def _():
        put(mine, of_self)
        put(other, of_neigh)

    @pl.when(core == 1)
    def _():
        put(other, of_self)
        put(mine, of_neigh)


def back_own_kernel(
    send,
    edge,
    spread,
    act,
    local,
    self_w,
    neigh_w,
    term0,
    term1,
    term2,
    term3,
    activated,
    back,
    self_w_out,
    neigh_w_out,
    place,
    send_now,
    sem,
):
    copy = pltpu.make_async_copy(send, send_now, sem.at[0])
    copy.start()
    over_rows = ((0,), (0,))
    width = NB * BS
    for r, term in enumerate((term0, term1, term2, term3)):
        of_round = edge[:, r * width : (r + 1) * width]
        term[...] = dot(of_round, spread[...], over_rows).astype(BF16)
    activated[...] = act[...]
    back[...] = dot(local[...], spread[...], over_rows)
    self_w_out[...] = self_w[...]
    neigh_w_out[...] = neigh_w[...]
    copy.wait()
    for i, r in enumerate(sent_rounds()):
        for s in range(NB):
            for b in range(BLK):
                at = (i * NB + s) * BLK + b
                hit = jnp.where(send_now[0, s, r] == b, 1.0, 0.0)
                place[at : at + 1, :] = jnp.full((1, BS), hit, F32)


def hid_part(k, size, self_w, neigh_w, low, back):
    at = rows(jnp.bitwise_xor(lax.axis_index("hid"), k), size)
    over_hidden = ((1,), (1,))
    return dot(self_w[at, :], low, over_hidden) + dot(neigh_w[at, :], back, over_hidden)


def back_kernel(
    place, start, low, self_w, neigh_w, got0, got1, got2, got3, own, far, give1, give3
):
    size, hidden = own.shape[0], start.shape[1]
    blocks = []
    for b in range(BLK):
        total = start[b * BS : (b + 1) * BS, :]
        for i, got in enumerate((got0, got1, got2, got3)):
            for s in range(NB):
                at = (i * NB + s) * BLK + b
                hit = jnp.concatenate([place[at : at + 1, :]] * (hidden // BS), axis=1)
                total = total + hit * got[s * BS : (s + 1) * BS, :].astype(F32)
        blocks.append(total.astype(BF16))
    back = jnp.concatenate(blocks, axis=0)
    part = functools.partial(hid_part, size=size, self_w=self_w, neigh_w=neigh_w)
    low_now = low[...]
    far[...] = part(2, low=low_now, back=back).astype(BF16)
    give1[...] = part(1, low=low_now, back=back).astype(BF16)
    give3[...] = part(3, low=low_now, back=back).astype(BF16)
    own[...] = part(0, low=low_now, back=back)


def on_device(
    features,
    self_weight,
    neigh_weight,
    cotangent,
    neighbor_blocks,
    local_tiles,
    send_blocks,
    recv_blocks,
    live_slots,
    boundary_tiles,
):
    n, width = features.shape
    hidden = self_weight.shape[1]
    slots = ROUNDS * NB * BS
    send_blocks = jnp.swapaxes(send_blocks, 1, 2)
    recv_blocks = jnp.swapaxes(recv_blocks, 1, 2)
    *packed, feats_now = call(
        pack_kernel,
        [((NB * BS // HID if r == 1 else NB * BS, width), BF16) for r in range(ROUNDS)]
        + [((n, width), BF16)],
        [HBM] * 2,
        nbytes=2_000_000,
        scratch=[pltpu.SMEM((1, NB, ROUNDS), jnp.int32), DMA((2,))],
    )(in_hbm(send_blocks), in_hbm(features))
    got_c, share, got_d, got_a = swaps(packed)
    (turned,) = call(
        turn_kernel, [((width, n), BF16)], [VMEM], flops=COVER_FLOPS, nbytes=2_000_000
    )(feats_now)
    share, got_a, turned = lax.optimization_barrier((share, got_a, turned))
    shares = [share] + [hid_swap(share, k) for k in (3, 1, 2)]
    local, edge, local_sum, inverse, own_pre = call(
        before_kernel,
        [
            ((n, n), BF16),
            ((n, slots), BF16),
            ((n, width), F32),
            ((n, BS), F32),
            ((n, hidden), F32),
        ],
        [HBM] * 6 + [VMEM] * 2,
        flops=COVER_FLOPS,
        nbytes=6_000_000,
        scratch=[
            pltpu.SMEM((1, BLK, K_IN), jnp.int32),
            pltpu.SMEM((1, NB, ROUNDS), jnp.int32),
            pltpu.SMEM((1, ROUNDS), jnp.int32),
            pltpu.VMEM((width, hidden), BF16),
            pltpu.VMEM((1, BLK, K_IN, BS, BS), BF16),
            pltpu.VMEM((1, ROUNDS, NB, BS, BS), BF16),
            DMA((6,)),
        ],
    )(
        in_hbm(neighbor_blocks),
        in_hbm(recv_blocks),
        in_hbm(live_slots),
        in_hbm(self_weight),
        in_hbm(local_tiles),
        in_hbm(boundary_tiles),
        feats_now,
        got_a,
    )
    act, low, spread, mean, give = call(
        middle_kernel,
        [((n, hidden), BF16)] * 3 + [((n, width), BF16), ((width, hidden), BF16)],
        [VMEM] * 13,
        flops=1_600_000_000,
        nbytes=8_000_000,
        scratch=[pltpu.VMEM((NB * BS, width), BF16)],
        limit=16,
    )(edge, got_c, got_d, *shares, local_sum, inverse, own_pre, neigh_weight, cotangent, turned)

    got = dom_swap(give, 1)
    (keep,) = call(
        keep_kernel, [((width, hidden), F32)], [VMEM] * 3, flops=200_000_000, nbytes=2_000_000
    )(turned, mean, low)
    got, keep = lax.optimization_barrier((got, keep))
    pieces = (CHIPS,) + PIECE
    (cut,) = call(cut_kernel, [(pieces, BF16)], [VMEM] * 2, nbytes=1_500_000)(keep, got)
    cut, spread, low = lax.optimization_barrier((cut, spread, low))
    *terms, activated, back, self_now, neigh_now, place = call(
        back_own_kernel,
        [((NB * BS, hidden), BF16)] * ROUNDS
        + [((n, hidden), BF16), ((n, hidden), F32)]
        + [((width, hidden), BF16)] * 2
        + [((ROUNDS * NB * BLK, BS), F32)],
        [HBM] + [VMEM] * 6,
        flops=600_000_000,
        nbytes=3_000_000,
        scratch=[pltpu.SMEM((1, NB, ROUNDS), jnp.int32), DMA((1,))],
    )(in_hbm(send_blocks), edge, spread, act, local, self_weight, neigh_weight)
    returned = swaps(terms)
    (summed,) = call(sum_kernel, [(pieces, BF16)], [VMEM], nbytes=700_000)(exchange(cut))
    summed, back = lax.optimization_barrier((summed, back))
    shape = (width // HID, n)
    in_own, in_far, in_first, in_third = call(
        back_kernel,
        [(shape, F32)] + [(shape, BF16)] * 3,
        [VMEM] * 9,
        flops=COVER_FLOPS,
        nbytes=3_000_000,
    )(place, back, low, self_now, neigh_now, *returned)
    in_parts = [hid_swap(in_far, 2), hid_swap(in_first, 1), hid_swap(in_third, 3)]
    mine = exchange(summed)
    other = dom_swap(mine, 1)
    scale = 1.0 / math.sqrt(n * lax.axis_size("dom"))
    grad_self, grad_neigh = call(
        functools.partial(last_kernel, scale),
        [((width, hidden), F32)] * 2,
        [VMEM] * 2,
        nbytes=2_000_000,
    )(mine, other)
    grad_input = in_own
    for part in in_parts:
        grad_input = grad_input + part.astype(F32)
    return activated, grad_self, grad_neigh, grad_input.astype(BF16).T


def solution(mesh):
    return jax.shard_map(
        on_device,
        mesh=mesh,
        in_specs=(
            P("dom", None),
            P(None, "hid"),
            P(None, "hid"),
            P("dom", "hid"),
            P("dom", None, None),
            P("dom", None, None, None, None),
            P("dom", None, None),
            P("dom", None, None),
            P("dom", None),
            P("dom", None, None, None, None),
        ),
        out_specs=(P("dom", "hid"), P(None, "hid"), P(None, "hid"), P("dom", "hid")),
        check_vma=False,
    )
```
